32 devices in a mesh: grp: 2 (over y), ctx: 4 (over x, core), head: 4 (over z).
Axes of the slice: x: 2, y: 2, z: 4, core: 2. Of those that a mesh axis runs over, the one named last changes fastest.
Arguments:
- prompt_hidden: bfloat16 [4, 1024, 4096], P('grp', 'ctx', 'head'), parts along dimension 0, may hold values from -3 to 3
- qkv_weight: bfloat16 [3, 4096, 4096], P(None, 'ctx', 'head'), may hold values from -0.09375 to 0.09375
- out_weight: bfloat16 [4096, 4096], P('head', 'ctx'), may hold values from -0.9375 to 0.9375
- embed_table: bfloat16 [32768, 4096], P('ctx', 'head'), may hold values from -60 to 60
- response_ids: int32 [4, 256], P(None, 'grp'), parts along dimension 1, may hold values from 0 to 32767
- assignment: int32 [256], P('grp'), parts along dimension 0, may hold values from 0 to 1
Outputs:
- final_hidden: bfloat16 [4, 256, 4096], P(None, ('grp', 'ctx'), 'head'), parts along dimension 1
The draws below stay inside these ranges and needn't reach their ends.
There are 2 independent parts, one for each index of `grp`. The reference program is written for one: setup_inputs(seed, part) draws one part's arguments, and reference() takes and returns one part's arrays. A program takes and returns all parts, laid end to end along the dimension named above; an argument that names none is the same for every part. Nothing has to cross between parts.
All inputs are finite; a program needn't handle non-finite values.
Results may differ from the reference program's by a relative error of at most 0.023.
Values may be sent and summed in bfloat16 or wider, within the bound.
No kernel may reach another device: no remote copies, remote signals or barrier semaphores. Data moves between devices by JAX's collectives and lax.ppermute only.
A program may use at most 128 MiB of HBM per device.

```python
import jax
import jax.numpy as jnp
from jax import lax

D = 4096
H = 32
VOCAB = 32768
DH = 128
STEPS = 4
PLEN = 1024
RESP = 128


def column_scale(key, width):
    position = jnp.arange(width, dtype=jnp.float32) / (width - 1)
    return (3.0 ** position)[None, :]


def draw_embed_table(key, part):
    base = jnp.clip(jax.random.normal(jax.random.fold_in(key, 3), (VOCAB, D), jnp.float32), -4.0, 4.0)
    return (base * column_scale(jax.random.fold_in(key, 5), D)).astype(jnp.bfloat16)


def draw_out_weight(key, part):
    base = jnp.clip(jax.random.normal(jax.random.fold_in(key, 11), (D, D), jnp.float32), -4.0, 4.0)
    scaled = base * column_scale(jax.random.fold_in(key, 13), D) / jnp.sqrt(jnp.float32(D))
    return jnp.clip(scaled, -0.9375, 0.9375).astype(jnp.bfloat16)


def set_ends(array, rng, low, top_value):
    extent = array.shape
    place = [jax.random.randint(jax.random.fold_in(rng, axis), (), 0, extent[axis]) for axis in range(len(extent))]
    array = array.at[tuple(place)].set(low)
    longest = extent.index(max(extent))
    place[longest] = (place[longest] + 1) % extent[longest]
    return array.at[tuple(place)].set(top_value)


def levels(own_key, shape, split, least, high):
    factor_of, own = 1.0, jax.random.fold_in(own_key, 6)
    for dim, blocks in split:
        heights = jnp.exp(jax.random.uniform(jax.random.fold_in(own, dim), (blocks,), jnp.float32, least / len(split), high / len(split)))
        factor_of = factor_of * jnp.repeat(heights, shape[dim] // blocks).reshape([-1 if axis == dim else 1 for axis in range(len(shape))])
    return factor_of


def scatter_about(own_key, dims, spread, reach, pieces=(), kind=jnp.bfloat16):
    loudness = levels(own_key, dims, pieces, -0.22, 0.18) if pieces else 1.0
    drawn = jax.random.normal(own_key, dims, jnp.float32) * spread * loudness
    return jnp.minimum(jnp.maximum(drawn, -reach), reach).astype(kind)


def setup_inputs(seed: int = 0, part: int = 0) -> dict:
    arg_keys = jax.random.split(jax.random.key(seed), 7)
    part_splits = jax.random.split(jax.random.fold_in(arg_keys[6], part), 7)
    prompt_hidden = scatter_about(part_splits[0], (2, PLEN, D), 0.5, 3.0, ((1, 4), (2, 4)))
    qkv_weight = scatter_about(arg_keys[1], (3, D, D), D ** -0.5, 0.09375, ((1, 4), (2, 4)))
    out_weight = draw_out_weight(jax.random.fold_in(arg_keys[6], 71), part)
    embed_table = draw_embed_table(jax.random.fold_in(arg_keys[6], 71), part)
    response_ids = set_ends(jax.random.randint(part_splits[4], (STEPS, RESP), 0, VOCAB), jax.random.fold_in(part_splits[4], 1), 0, VOCAB - 1).astype(jnp.int32)
    assignment = set_ends(jax.random.randint(part_splits[5], (RESP,), 0, 2), jax.random.fold_in(part_splits[5], 1), 0, 1).astype(jnp.int32)
    return {"prompt_hidden": prompt_hidden, "qkv_weight": qkv_weight, "out_weight": out_weight, "embed_table": embed_table, "response_ids": response_ids, "assignment": assignment}


def rms_rows(values):
    return values * lax.rsqrt(lax.optimization_barrier(jnp.mean(values * values, axis=-1, keepdims=True)) + 1e-06)

def reference(prompt_hidden, qkv_weight, out_weight, embed_table, response_ids, assignment):
    kv_weight = jnp.concatenate([qkv_weight[1], qkv_weight[2]], axis=1)
    rows = prompt_hidden.reshape(2 * PLEN, D)
    kv_all = jnp.dot(rows, kv_weight, preferred_element_type=jnp.float32).astype(jnp.bfloat16)
    kv_all = kv_all.reshape(2, PLEN, 2, H, DH)
    keys = kv_all[:, :, 0].astype(jnp.float32)
    values = kv_all[:, :, 1].astype(jnp.float32)
    state = jnp.einsum('pthd,pthe->phde', keys, values)
    embedded = jnp.take(embed_table, response_ids, axis=0)
    normed = rms_rows(embedded.astype(jnp.float32)).astype(jnp.bfloat16)
    flat = normed.reshape(STEPS * RESP, D)
    query = jnp.dot(flat, qkv_weight[0], preferred_element_type=jnp.float32).astype(jnp.bfloat16).reshape(STEPS, RESP, H, DH)
    key = jnp.dot(flat, qkv_weight[1], preferred_element_type=jnp.float32).astype(jnp.bfloat16).reshape(STEPS, RESP, H, DH)
    value = jnp.dot(flat, qkv_weight[2], preferred_element_type=jnp.float32).astype(jnp.bfloat16).reshape(STEPS, RESP, H, DH)
    query_f = query.astype(jnp.float32)
    both = jnp.einsum('trhd,phde->ptrhe', query_f, state, precision=lax.Precision.HIGHEST)
    chosen = jnp.where((assignment == 0)[None, :, None, None], both[0], both[1])
    scores = jnp.einsum('trhd,srhd->rhts', query_f, key.astype(jnp.float32))
    later = jnp.arange(STEPS)[:, None] >= jnp.arange(STEPS)[None, :]
    scores = jnp.where(later[None, None], scores, 0.0).astype(jnp.bfloat16)
    local = jnp.einsum('rhts,srhd->trhd', scores.astype(jnp.float32), value.astype(jnp.float32))
    attended = chosen + local
    head_out = rms_rows(attended).astype(jnp.bfloat16).reshape(STEPS * RESP, D)
    projected = jnp.dot(head_out, out_weight, preferred_element_type=jnp.float32).reshape(STEPS, RESP, D)
    mixed = embedded.astype(jnp.float32) + projected
    return rms_rows(mixed).astype(jnp.bfloat16)
```

```python
import functools

import jax
import jax.numpy as jnp
from jax import lax
from jax.experimental import pallas as pl
from jax.experimental.pallas import tpu as pltpu
from jax.sharding import PartitionSpec as P

DH = 128
F32 = jnp.float32
BF16 = jnp.bfloat16
VMEM_LIMIT = 48 * 1024 * 1024


def rms_rows(values):
    return values * lax.rsqrt(jnp.mean(values * values, axis=-1, keepdims=True) + 1e-06)


def gathered_plan(prompt_hidden, qkv_weight, out_weight, embed_table, response_ids, assignment):
    local_cols = prompt_hidden.shape[2]
    prompt_rows = prompt_hidden.shape[1]
    head_size = DH
    local_heads = local_cols // head_size
    steps = response_ids.shape[0]
    resp_local = response_ids.shape[1] // lax.axis_size("ctx")
    ctx_index = lax.axis_index("ctx")
    full_rows = lax.all_gather(qkv_weight, "ctx", axis=1, tiled=True)
    kv_weight = jnp.concatenate([full_rows[1], full_rows[2]], axis=1)
    piece = lax.all_gather(prompt_hidden, "head", axis=2, tiled=True)
    flat_piece = piece.reshape(2 * prompt_rows, piece.shape[2])
    kv_local = jnp.dot(flat_piece, kv_weight, preferred_element_type=jnp.float32)
    kv_local = kv_local.astype(jnp.bfloat16).reshape(2, prompt_rows, 2, local_heads, head_size)
    partial_state = jnp.einsum(
        "pthd,pthe->phde", kv_local[:, :, 0], kv_local[:, :, 1], preferred_element_type=jnp.float32
    )
    state = lax.psum(partial_state.astype(jnp.bfloat16), "ctx").astype(jnp.float32)
    vocab_rows = embed_table.shape[0]
    offset_ids = response_ids - ctx_index * vocab_rows
    inside = (offset_ids >= 0) & (offset_ids < vocab_rows)
    looked = jnp.take(embed_table, jnp.clip(offset_ids, 0, vocab_rows - 1), axis=0)
    looked = jnp.where(inside[:, :, None], looked.astype(jnp.float32), 0.0)
    embedded_mine = lax.psum_scatter(
        looked.astype(jnp.bfloat16), "ctx", scatter_dimension=1, tiled=True
    )
    embedded = lax.all_gather(embedded_mine, "head", axis=2, tiled=True)
    normed = rms_rows(embedded.astype(jnp.float32)).astype(jnp.bfloat16)
    projected_qkv = jnp.einsum(
        "trd,kde->trke", normed, full_rows, preferred_element_type=jnp.float32
    ).astype(jnp.bfloat16)
    projected_qkv = projected_qkv.reshape(steps, resp_local, 3, local_heads, head_size)
    query = projected_qkv[:, :, 0]
    key = projected_qkv[:, :, 1]
    value = projected_qkv[:, :, 2]
    my_prompt = lax.dynamic_slice_in_dim(assignment, ctx_index * resp_local, resp_local, 0)
    query_f = query.astype(jnp.float32)
    both = jnp.einsum("trhd,phde->ptrhe", query_f, state, precision=lax.Precision.HIGHEST)
    chosen = jnp.where((my_prompt == 0)[None, :, None, None], both[0], both[1])
    scores = jnp.einsum("trhd,srhd->rhts", query, key, preferred_element_type=jnp.float32)
    later = jnp.arange(steps)[:, None] >= jnp.arange(steps)[None, :]
    scores = jnp.where(later[None, None], scores, 0.0).astype(jnp.bfloat16)
    local = jnp.einsum("rhts,srhd->trhd", scores, value, preferred_element_type=jnp.float32)
    head_out = rms_rows(chosen + local).astype(jnp.bfloat16).reshape(steps, resp_local, local_cols)
    terms = jnp.einsum(
        "trd,de->tre",
        head_out,
        lax.all_gather(out_weight, "ctx", axis=1, tiled=True),
        preferred_element_type=jnp.float32,
    )
    width = terms.shape[2]
    mine = lax.psum_scatter(
        terms.astype(jnp.bfloat16), "head", scatter_dimension=2, tiled=True
    ).astype(jnp.float32)
    mixed = embedded_mine.astype(jnp.float32) + mine
    squares = lax.psum(jnp.sum(mixed * mixed, axis=-1), "head")
    result = mixed * lax.rsqrt(squares[:, :, None] / width + 1e-06)
    return result.astype(jnp.bfloat16)


def permute(array, axis, pairs):
    return lax.ppermute(array, axis, pairs)


def xor_pairs(count, mask):
    return [(i, i ^ mask) for i in range(count)]


def shift_pairs(count, by):
    return [(i, (i + by) % count) for i in range(count)]


def fetch_rows(meta, blocks, held, sems, parts):
    depth = held.shape[2]
    copies = []
    for part in range(parts):
        for k in range(len(blocks) // parts):
            block = blocks[part * (len(blocks) // parts) + k]
            rows = block.shape[0]
            for s in range(2):
                copies.append(
                    pltpu.make_async_copy(
                        block.at[:, pl.ds(s * depth, depth)],
                        held.at[2 * meta[k] + s, pl.ds(part * rows, rows), :],
                        sems.at[len(copies)],
                    )
                )
    for copy in copies:
        copy.start()
    for copy in copies:
        copy.wait()


def weight_slices(own, sib, crossed, depth):
    parts = [own[pl.ds(0, depth), :], own[pl.ds(depth, depth), :]]
    parts += [sib[pl.ds(0, depth), :], sib[pl.ds(depth, depth), :]]
    return parts + [ref[...] for ref in crossed]


def slot_dot(meta, first, held, parts):
    total = None
    for i, part in enumerate(parts):
        term = jnp.dot(held[meta[first + i]], part, preferred_element_type=F32)
        total = term if total is None else total + term
    return total


def state_kernel(nblocks, meta, *refs):
    blocks, refs = refs[:nblocks], refs[nblocks:]
    key_own, value_own, key_sib, value_sib = refs[:4]
    key_far, value_far = refs[4:8], refs[8:12]
    out, rounded, held, sems = refs[12:]
    depth = held.shape[2]

    @pl.when(pl.program_id(0) == 0)
    def _():
        fetch_rows(meta, blocks, held, sems, 2)

    first = nblocks // 2
    keys = slot_dot(meta, first, held, weight_slices(key_own.at[0], key_sib.at[0], key_far, depth)).astype(BF16)
    values = slot_dot(meta, first, held, weight_slices(value_own.at[0], value_sib.at[0], value_far, depth)).astype(BF16)
    for head in range(out.shape[0]):
        cols = slice(head * DH, (head + 1) * DH)
        state = lax.dot_general(
            keys[:, cols], values[:, cols], (((0,), (0,)), ((), ())), preferred_element_type=F32
        )
        out[head] = state
        rounded[head] = state.astype(BF16)


def project_kernel(nblocks, steps, meta, *refs):
    blocks, refs = refs[:nblocks], refs[nblocks:]
    own, sib = refs[:3], refs[3:6]
    far = refs[6:10], refs[10:14], refs[14:18]
    query_out, local_out, held, sems = refs[18:]
    slots, rows, depth = held.shape

    @pl.when(pl.program_id(0) == 0)
    def _():
        fetch_rows(meta, blocks, held, sems, 2)
        squares = jnp.zeros((rows, 1), F32)
        for i in range(slots):
            part = held[i].astype(F32)
            squares += jnp.sum(part * part, axis=-1, keepdims=True)
        scale = lax.rsqrt(squares / (slots * depth) + 1e-06)
        for i in range(slots):
            held[i] = (held[i].astype(F32) * scale).astype(BF16)

    first = nblocks // 2
    query, key, value = (
        slot_dot(meta, first, held, weight_slices(own[i].at[0], sib[i].at[0], far[i], depth)).astype(BF16)
        for i in range(3)
    )
    query_out[...] = query
    query, key, value = query.astype(F32), key.astype(F32), value.astype(F32)
    each = rows // 2 // steps
    for part in range(2):
        for s in range(steps):
            at_s = slice((part * steps + s) * each, (part * steps + s + 1) * each)
            for head in range(query.shape[1] // DH):
                cols = slice(head * DH, (head + 1) * DH)
                total = None
                for u in range(s + 1):
                    at_u = slice((part * steps + u) * each, (part * steps + u + 1) * each)
                    score = jnp.sum(query[at_s, cols] * key[at_u, cols], axis=-1, keepdims=True)
                    term = score.astype(BF16).astype(F32) * value[at_u, cols]
                    total = term if total is None else total + term
                local_out[at_s, cols] = total


def attend_kernel(query, local, chosen, state0, state1, other0, other1, out):
    second = chosen[...] != 0
    for head in range(state0.shape[0]):
        cols = slice(head * DH, (head + 1) * DH)
        q = query[:, cols]
        both = []
        for mine, other in ((state0, other0), (state1, other1)):
            state = mine[head] + other[head].astype(F32)
            high = state.astype(BF16)
            low = (state - high.astype(F32)).astype(BF16)
            both.append(
                jnp.dot(q, high, preferred_element_type=F32) + jnp.dot(q, low, preferred_element_type=F32)
            )
        attended = jnp.where(second, both[1], both[0]) + local[:, cols]
        out[:, cols] = rms_rows(attended).astype(BF16)


def output_kernel(npieces, meta, heads_own, heads_sib, *refs):
    pieces, refs = refs[:npieces], refs[npieces:]
    outs, refs = refs[:4], refs[4:]
    held, terms, sems = refs
    rows, width = held.shape[1:]
    core = meta[4]
    copies = []
    copies.append([pltpu.make_async_copy(pieces[0], held.at[0], sems.at[0])])
    copies.append([pltpu.make_async_copy(pieces[1], held.at[1], sems.at[1])])
    for j in (2, 3):
        pair = []
        for s in range(2):
            i = 2 + (j - 2) * 2 + s
            at = pl.multiple_of(meta[5 + s] * (rows // 2), rows // 2)
            pair.append(pltpu.make_async_copy(pieces[i], held.at[j, pl.ds(at, rows // 2), :], sems.at[i]))
        copies.append(pair)
    for pair in copies:
        for copy in pair:
            copy.start()
    half = rows // 2
    own_at = pl.multiple_of(core * half, half)
    sib_at = pl.multiple_of((1 - core) * half, half)
    for j in range(4):
        for copy in copies[j]:
            copy.wait()
        term = jnp.dot(heads_own[...], held[j, pl.ds(own_at, half), :], preferred_element_type=F32)
        term += jnp.dot(heads_sib[...], held[j, pl.ds(sib_at, half), :], preferred_element_type=F32)
        terms[meta[j]] = term
    for k in range(4):
        outs[k][...] = terms[k].astype(outs[k].dtype)


def anywhere(count):
    return [pl.BlockSpec(memory_space=pl.ANY)] * count


def permuted_plan(prompt_hidden, qkv_weight, out_weight, embed_table, response_ids, assignment):
    grp, ctx, head = lax.axis_index("grp"), lax.axis_index("ctx"), lax.axis_index("head")
    nctx, nhead = lax.axis_size("ctx"), lax.axis_size("head")
    core, chip = ctx % 2, ctx // 2
    to_sib, to_far, to_diag = xor_pairs(nctx, 1), xor_pairs(nctx, 2), xor_pairs(nctx, 3)
    over_grp = xor_pairs(2, 1)
    ring = shift_pairs(nhead, 1)
    prompts, prompt_rows, block = prompt_hidden.shape
    depth = block // 2
    cols = qkv_weight.shape[2] // 2
    steps = response_ids.shape[0]
    resp_local = response_ids.shape[1] // nctx
    rows_local = steps * resp_local

    def half_slice(k, col_half):
        return lax.dynamic_slice(qkv_weight, (k, grp * depth, col_half * cols), (1, depth, cols))[0]

    order = [(k, mask) for k in (1, 2) for mask in (2, 3)]
    sent = lax.optimization_barrier(
        tuple(half_slice(k, core if mask == 2 else 1 - core) for k, mask in order)
    )
    crossed = {}
    for (k, mask), part in zip(order, sent):
        got = permute(part, "ctx", to_far if mask == 2 else to_diag)
        crossed[k, mask] = (got, permute(got, "grp", over_grp))
    sib_weight = permute(
        lax.dynamic_slice(qkv_weight, (0, 0, (1 - core) * cols), (3, block, cols)), "ctx", to_sib
    )

    own_blocks, sib_blocks = [], []
    for p in range(prompts):
        moving = prompt_hidden[p]
        own, sib = [moving], [permute(moving, "ctx", to_sib)]
        for _ in range(nhead - 1):
            moving = permute(moving, "head", ring)
            own.append(moving)
            sib.append(permute(moving, "ctx", to_sib))
        own_blocks.append(own)
        sib_blocks.append(sib)

    vocab_rows = embed_table.shape[0]
    offset_ids = response_ids - ctx * vocab_rows
    inside = (offset_ids >= 0) & (offset_ids < vocab_rows)
    looked = jnp.take(embed_table, jnp.clip(offset_ids, 0, vocab_rows - 1), axis=0)
    looked = jnp.where(inside[:, :, None], looked, jnp.zeros((), BF16))
    looked = looked.reshape(steps, nctx // 2, 2, resp_local, block)
    kept = lax.dynamic_index_in_dim(looked, core, 2, keepdims=False)
    given = lax.dynamic_index_in_dim(looked, 1 - core, 2, keepdims=False)
    kept = kept + permute(given, "ctx", to_sib)
    mine = lax.dynamic_index_in_dim(kept, chip, 1, keepdims=False)
    given = lax.dynamic_index_in_dim(kept, 1 - chip, 1, keepdims=False)
    embedded = (mine + permute(given, "ctx", to_far)).reshape(rows_local, block)
    moving = embedded
    own_rows, sib_rows = [moving], [permute(moving, "ctx", to_sib)]
    for _ in range(nhead - 1):
        moving = permute(moving, "head", ring)
        own_rows.append(moving)
        sib_rows.append(permute(moving, "ctx", to_sib))

    for mask in (2, 3):
        part = half_slice(0, core if mask == 2 else 1 - core)
        part, _ = lax.optimization_barrier((part, given))
        got = permute(part, "ctx", to_far if mask == 2 else to_diag)
        crossed[0, mask] = (got, permute(got, "grp", over_grp))
    out_sib = permute(out_weight, "ctx", to_sib)
    part = lax.dynamic_slice(out_weight, (grp * depth, 0), (depth, out_weight.shape[1]))
    part, _ = lax.optimization_barrier((part, crossed[2, 3][0]))
    got = permute(part, "ctx", to_far)
    out_far = (got, permute(got, "grp", over_grp))
    out_diag = tuple(permute(piece, "ctx", to_sib) for piece in out_far)

    slots = [(head - k) % nhead for k in range(nhead)]
    for j in range(nctx):
        if j < 2:
            slots += [2 * (ctx ^ j), 2 * (ctx ^ j) + 1]
        else:
            slots += [2 * (ctx ^ j) + grp, 2 * (ctx ^ j) + 1 - grp]
    meta = jnp.stack(slots + [core]).astype(jnp.int32)
    at_core = len(slots)
    wide = 2 * DH
    nsteps = cols // wide

    def own_spec(k):
        return pl.BlockSpec((1, block, wide), lambda n, m: (k, 0, m[at_core] * nsteps + n))

    def sib_spec(k):
        return pl.BlockSpec((1, block, wide), lambda n, m: (k, 0, n))

    far_spec = pl.BlockSpec((depth, wide), lambda n, m: (0, n))
    far_of = lambda k: [*crossed[k, 2], *crossed[k, 3]]
    nblocks = 2 * nhead
    heads_here = cols // DH
    tokens = 2 * prompt_rows

    states, rounded = [], []
    for p in range(prompts):
        state_spec = pl.BlockSpec((2, DH, DH), lambda n, m: (n, 0, 0))
        state, low = pl.pallas_call(
            functools.partial(state_kernel, nblocks),
            out_shape=(
                jax.ShapeDtypeStruct((heads_here, DH, DH), F32),
                jax.ShapeDtypeStruct((heads_here, DH, DH), BF16),
            ),
            grid_spec=pltpu.PrefetchScalarGridSpec(
                num_scalar_prefetch=1,
                grid=(nsteps,),
                in_specs=anywhere(nblocks)
                + [own_spec(1), own_spec(2), sib_spec(1), sib_spec(2)]
                + [far_spec] * 8,
                out_specs=(state_spec, state_spec),
                scratch_shapes=[
                    pltpu.VMEM((2 * nhead, tokens, depth), BF16),
                    pltpu.SemaphoreType.DMA((2 * nblocks,)),
                ],
            ),
            compiler_params=pltpu.CompilerParams(vmem_limit_bytes=VMEM_LIMIT),
            cost_estimate=pl.CostEstimate(
                flops=4 * tokens * nhead * block * cols, bytes_accessed=12 * 1024 * 1024, transcendentals=0
            ),
            name="prompt_state",
        )(
            meta,
            *own_blocks[p],
            *sib_blocks[p],
            qkv_weight,
            qkv_weight,
            sib_weight,
            sib_weight,
            *far_of(1),
            *far_of(2),
        )
        states.append(state)
        rounded.append(permute(low, "ctx", to_far))

    chip_rows = 2 * rows_local
    row_spec = pl.BlockSpec((chip_rows, wide), lambda n, m: (0, n))
    query, local = pl.pallas_call(
        functools.partial(project_kernel, nblocks, steps),
        out_shape=(
            jax.ShapeDtypeStruct((chip_rows, cols), BF16),
            jax.ShapeDtypeStruct((chip_rows, cols), F32),
        ),
        grid_spec=pltpu.PrefetchScalarGridSpec(
            num_scalar_prefetch=1,
            grid=(nsteps,),
            in_specs=anywhere(nblocks)
            + [own_spec(0), own_spec(1), own_spec(2), sib_spec(0), sib_spec(1), sib_spec(2)]
            + [far_spec] * 12,
            out_specs=(row_spec, row_spec),
            scratch_shapes=[
                pltpu.VMEM((2 * nhead, chip_rows, depth), BF16),
                pltpu.SemaphoreType.DMA((2 * nblocks,)),
            ],
        ),
        compiler_params=pltpu.CompilerParams(vmem_limit_bytes=VMEM_LIMIT),
        cost_estimate=pl.CostEstimate(
            flops=6 * chip_rows * nhead * block * cols, bytes_accessed=14 * 1024 * 1024, transcendentals=0
        ),
        name="response_rows",
    )(
        meta,
        *own_rows,
        *sib_rows,
        *([qkv_weight] * 3),
        *([sib_weight] * 3),
        *far_of(0),
        *far_of(1),
        *far_of(2),
    )

    which = [
        jnp.tile(lax.dynamic_slice_in_dim(assignment, owner * resp_local, resp_local, 0), steps)
        for owner in (ctx, ctx ^ 1)
    ]
    heads_out = pl.pallas_call(
        attend_kernel,
        out_shape=jax.ShapeDtypeStruct((chip_rows, cols), BF16),
        compiler_params=pltpu.CompilerParams(vmem_limit_bytes=VMEM_LIMIT),
        name="attend",
    )(query, local, jnp.concatenate(which)[:, None], *states, *rounded)

    heads_own = heads_out[:rows_local]
    heads_sib = permute(heads_out[rows_local:], "ctx", to_sib)

    away = [((ctx ^ j) - head) % nhead for j in range(nctx)]
    out_meta = jnp.stack(away + [core, grp, 1 - grp]).astype(jnp.int32)
    width = out_weight.shape[1]
    whole = pl.BlockSpec((rows_local, cols), lambda i, m: (0, 0))
    term_spec = pl.BlockSpec((rows_local, width), lambda i, m: (0, 0))
    terms = pl.pallas_call(
        functools.partial(output_kernel, 6),
        out_shape=(jax.ShapeDtypeStruct((rows_local, width), F32),)
        + (jax.ShapeDtypeStruct((rows_local, width), BF16),) * 3,
        grid_spec=pltpu.PrefetchScalarGridSpec(
            num_scalar_prefetch=1,
            grid=(1,),
            in_specs=[whole, whole] + anywhere(6),
            out_specs=(term_spec,) * 4,
            scratch_shapes=[
                pltpu.VMEM((nctx, block, width), BF16),
                pltpu.VMEM((nctx, rows_local, width), F32),
                pltpu.SemaphoreType.DMA((6,)),
            ],
        ),
        compiler_params=pltpu.CompilerParams(vmem_limit_bytes=VMEM_LIMIT),
        name="output_terms",
    )(out_meta, heads_own, heads_sib, out_weight, out_sib, *out_far, *out_diag)
    mixed = embedded.astype(F32) + terms[0]
    for k in range(1, nhead):
        mixed = mixed + permute(terms[k], "head", shift_pairs(nhead, k)).astype(F32)
    squares = lax.psum(jnp.sum(mixed * mixed, axis=-1, keepdims=True), "head")
    result = mixed * lax.rsqrt(squares / (nhead * width) + 1e-06)
    return result.astype(BF16).reshape(steps, resp_local, width)


def on_device(prompt_hidden, qkv_weight, out_weight, embed_table, response_ids, assignment):
    nctx, nhead = lax.axis_size("ctx"), lax.axis_size("head")
    local_heads = qkv_weight.shape[2] // DH
    fits = (
        lax.axis_size("grp") == 2
        and nctx == 4
        and nhead == 4
        and prompt_hidden.shape[0] == 2
        and local_heads % 4 == 0
        and prompt_hidden.shape[1] % 16 == 0
        and (response_ids.shape[1] // nctx) % 16 == 0
    )
    plan = permuted_plan if fits else gathered_plan
    return plan(prompt_hidden, qkv_weight, out_weight, embed_table, response_ids, assignment)


def solution(mesh):
    return jax.shard_map(
        on_device,
        mesh=mesh,
        in_specs=(
            P("grp", "ctx", "head"),
            P(None, "ctx", "head"),
            P("head", "ctx"),
            P("ctx", "head"),
            P(None, "grp"),
            P("grp"),
        ),
        out_specs=P(None, ("grp", "ctx"), "head"),
        check_vma=False,
    )
```

```python
import functools

import jax
import jax.numpy as jnp
from jax import lax
from jax.experimental import pallas as pl
from jax.experimental.pallas import tpu as pltpu
from jax.sharding import PartitionSpec as P

DH = 128
F32 = jnp.float32
BF16 = jnp.bfloat16
VMEM_LIMIT = 56 * 1024 * 1024
VMEM_SMALL = 16 * 1024 * 1024


def rms_rows(values):
    return values * lax.rsqrt(jnp.mean(values * values, axis=-1, keepdims=True) + 1e-06)


def gathered_plan(prompt_hidden, qkv_weight, out_weight, embed_table, response_ids, assignment):
    local_cols = prompt_hidden.shape[2]
    prompt_rows = prompt_hidden.shape[1]
    head_size = DH
    local_heads = local_cols // head_size
    steps = response_ids.shape[0]
    resp_local = response_ids.shape[1] // lax.axis_size("ctx")
    ctx_index = lax.axis_index("ctx")
    full_rows = lax.all_gather(qkv_weight, "ctx", axis=1, tiled=True)
    kv_weight = jnp.concatenate([full_rows[1], full_rows[2]], axis=1)
    piece = lax.all_gather(prompt_hidden, "head", axis=2, tiled=True)
    flat_piece = piece.reshape(2 * prompt_rows, piece.shape[2])
    kv_local = jnp.dot(flat_piece, kv_weight, preferred_element_type=jnp.float32)
    kv_local = kv_local.astype(jnp.bfloat16).reshape(2, prompt_rows, 2, local_heads, head_size)
    partial_state = jnp.einsum(
        "pthd,pthe->phde", kv_local[:, :, 0], kv_local[:, :, 1], preferred_element_type=jnp.float32
    )
    state = lax.psum(partial_state.astype(jnp.bfloat16), "ctx").astype(jnp.float32)
    vocab_rows = embed_table.shape[0]
    offset_ids = response_ids - ctx_index * vocab_rows
    inside = (offset_ids >= 0) & (offset_ids < vocab_rows)
    looked = jnp.take(embed_table, jnp.clip(offset_ids, 0, vocab_rows - 1), axis=0)
    looked = jnp.where(inside[:, :, None], looked.astype(jnp.float32), 0.0)
    embedded_mine = lax.psum_scatter(
        looked.astype(jnp.bfloat16), "ctx", scatter_dimension=1, tiled=True
    )
    embedded = lax.all_gather(embedded_mine, "head", axis=2, tiled=True)
    normed = rms_rows(embedded.astype(jnp.float32)).astype(jnp.bfloat16)
    projected_qkv = jnp.einsum(
        "trd,kde->trke", normed, full_rows, preferred_element_type=jnp.float32
    ).astype(jnp.bfloat16)
    projected_qkv = projected_qkv.reshape(steps, resp_local, 3, local_heads, head_size)
    query = projected_qkv[:, :, 0]
    key = projected_qkv[:, :, 1]
    value = projected_qkv[:, :, 2]
    my_prompt = lax.dynamic_slice_in_dim(assignment, ctx_index * resp_local, resp_local, 0)
    query_f = query.astype(jnp.float32)
    both = jnp.einsum("trhd,phde->ptrhe", query_f, state, precision=lax.Precision.HIGHEST)
    chosen = jnp.where((my_prompt == 0)[None, :, None, None], both[0], both[1])
    scores = jnp.einsum("trhd,srhd->rhts", query, key, preferred_element_type=jnp.float32)
    later = jnp.arange(steps)[:, None] >= jnp.arange(steps)[None, :]
    scores = jnp.where(later[None, None], scores, 0.0).astype(jnp.bfloat16)
    local = jnp.einsum("rhts,srhd->trhd", scores, value, preferred_element_type=jnp.float32)
    head_out = rms_rows(chosen + local).astype(jnp.bfloat16).reshape(steps, resp_local, local_cols)
    terms = jnp.einsum(
        "trd,de->tre",
        head_out,
        lax.all_gather(out_weight, "ctx", axis=1, tiled=True),
        preferred_element_type=jnp.float32,
    )
    width = terms.shape[2]
    mine = lax.psum_scatter(
        terms.astype(jnp.bfloat16), "head", scatter_dimension=2, tiled=True
    ).astype(jnp.float32)
    mixed = embedded_mine.astype(jnp.float32) + mine
    squares = lax.psum(jnp.sum(mixed * mixed, axis=-1), "head")
    result = mixed * lax.rsqrt(squares[:, :, None] / width + 1e-06)
    return result.astype(jnp.bfloat16)


def permute(array, axis, pairs):
    return lax.ppermute(array, axis, pairs)


def xor_pairs(count, mask):
    return [(i, i ^ mask) for i in range(count)]


def shift_pairs(count, by):
    return [(i, (i + by) % count) for i in range(count)]


def fetch_rows(meta, blocks, parts, held, sems):
    count = len(blocks) // parts
    block = held.shape[1] // count
    copies = []
    for part in range(parts):
        for k in range(count):
            rows = blocks[part * count + k].shape[0]
            at = pl.multiple_of(meta[k] * block, block)
            copies.append(
                pltpu.make_async_copy(
                    blocks[part * count + k],
                    held.at[pl.ds(part * rows, rows), pl.ds(at, block)],
                    sems.at[len(copies)],
                )
            )
    for copy in copies:
        copy.start()
    for copy in copies:
        copy.wait()


def held_dot(held, weights):
    total, at = None, 0
    for weight in weights:
        term = jnp.dot(held[:, at : at + weight.shape[0]], weight, preferred_element_type=F32)
        total = term if total is None else total + term
        at += weight.shape[0]
    return total


def state_kernel(nblocks, meta, *refs):
    blocks, refs = refs[:nblocks], refs[nblocks:]
    key_own, value_own, key_sib, value_sib = refs[:4]
    key_far, value_far = refs[4:6], refs[6:8]
    out, rounded, held, sems = refs[8:]
    prompts = out.shape[0]
    half = nblocks // 2

    @pl.when(pl.program_id(0) == 0)
    def _():
        parts = [blocks[s * half + k].at[p] for p in range(prompts) for s in range(2) for k in range(half)]
        fetch_rows(meta, parts, 2 * prompts, held, sems)

    keys = [key_own[0], key_sib[0]] + [ref[...] for ref in key_far]
    values = [value_own[0], value_sib[0]] + [ref[...] for ref in value_far]
    parts = [jnp.concatenate(pair, axis=1) for pair in zip(keys, values)]
    both = held_dot(held, parts).astype(BF16)
    tokens = both.shape[0] // prompts
    for p in range(prompts):
        rows = both[p * tokens : (p + 1) * tokens]
        state = lax.dot_general(
            rows[:, :DH], rows[:, DH:], (((0,), (0,)), ((), ())), preferred_element_type=F32
        )
        out[p, 0] = state
        rounded[p, 0] = state.astype(BF16)


def project_kernel(nhead, steps, meta, mine, other, *refs):
    own, sib = refs[:3], refs[3:6]
    far = refs[6:8], refs[8:10], refs[10:12]
    query_out, local_out, residual, held, sems = refs[12:]
    rows, features = held.shape
    depth = features // (2 * nhead)

    @pl.when(pl.program_id(0) == 0)
    def _():
        fetch_rows(meta, [ref.at[k] for ref in (mine, other) for k in range(nhead)], 2, held, sems)
        share = residual.shape[0]
        at = pl.multiple_of(meta[nhead] * share, share)
        residual[...] = held[pl.ds(at, share), :]
        squares = jnp.zeros((rows, 1), F32)
        for i in range(0, features, depth):
            part = held[:, i : i + depth].astype(F32)
            squares += jnp.sum(part * part, axis=-1, keepdims=True)
        scale = lax.rsqrt(squares / features + 1e-06)
        for i in range(0, features, depth):
            held[:, i : i + depth] = (held[:, i : i + depth].astype(F32) * scale).astype(BF16)

    query, key, value = (
        held_dot(held, [own[i][0], sib[i][0]] + [ref[...] for ref in far[i]]).astype(BF16) for i in range(3)
    )
    query_out[...] = query
    query, key, value = query.astype(F32), key.astype(F32), value.astype(F32)
    each = rows // 2 // steps
    for part in range(2):
        for s in range(steps):
            at_s = slice((part * steps + s) * each, (part * steps + s + 1) * each)
            for head in range(query.shape[1] // DH):
                cols = slice(head * DH, (head + 1) * DH)
                total = None
                for u in range(s + 1):
                    at_u = slice((part * steps + u) * each, (part * steps + u + 1) * each)
                    score = jnp.sum(query[at_s, cols] * key[at_u, cols], axis=-1, keepdims=True)
                    term = score.astype(BF16).astype(F32) * value[at_u, cols]
                    total = term if total is None else total + term
                local_out[at_s, cols] = total


def attend_kernel(query, local, chosen, states, others, out, given):
    second = chosen[...] != 0
    rows = out.shape[0]
    for head in range(states.shape[1]):
        cols = slice(head * DH, (head + 1) * DH)
        q = query[:, cols]
        both = []
        for p in range(2):
            state = states[p, head] + others[p, head].astype(F32)
            high = state.astype(BF16)
            low = (state - high.astype(F32)).astype(BF16)
            both.append(
                jnp.dot(q, high, preferred_element_type=F32) + jnp.dot(q, low, preferred_element_type=F32)
            )
        attended = jnp.where(second, both[1], both[0]) + local[:, cols]
        normed = rms_rows(attended).astype(BF16)
        out[:, cols] = normed[:rows]
        given[:, cols] = normed[rows:]


def share_out(meta, terms, outs):
    for k, out in enumerate(outs):
        share = out.shape[0]
        at = pl.multiple_of(meta[k] * share, share)
        out[...] = terms[pl.ds(at, share), :].astype(out.dtype)


def near_kernel(meta, heads_own, heads_sib, own, sib, *refs):
    outs, terms = refs[:-1], refs[-1]
    core = meta[len(outs)]
    half, width = heads_own.shape[1], own.shape[1]
    own_at = pl.multiple_of(core * half, half)
    sib_at = pl.multiple_of((1 - core) * half, half)
    for j, weight in enumerate((own, sib)):
        term = jnp.dot(heads_own[...], weight[pl.ds(own_at, half), :], preferred_element_type=F32)
        term += jnp.dot(heads_sib[...], weight[pl.ds(sib_at, half), :], preferred_element_type=F32)
        terms[:, j * width : (j + 1) * width] = term
    share_out(meta, terms, outs)


def far_kernel(meta, heads_own, heads_sib, far_x, far_y, diag_x, diag_y, *refs):
    outs, heads, terms = refs[:-2], refs[-2], refs[-1]
    core, group = meta[len(outs)], meta[len(outs) + 1]
    heads[core] = heads_own[...]
    heads[1 - core] = heads_sib[...]
    width = far_x.shape[1]
    for i, (first, second) in enumerate(((far_x, far_y), (diag_x, diag_y))):
        term = jnp.dot(heads[group], first[...], preferred_element_type=F32)
        term += jnp.dot(heads[1 - group], second[...], preferred_element_type=F32)
        at = pl.multiple_of((i ^ group) * width, width)
        terms[:, pl.ds(at, width)] = term
    share_out(meta, terms, outs)


def norm_kernel(nhead, meta, residual, *refs):
    near, far, outs, mixed = refs[:nhead], refs[nhead : 2 * nhead], refs[2 * nhead : 3 * nhead], refs[-1]
    part = near[0].shape[1]
    squares = 0.0
    for i, group in enumerate((near, far)):
        total = residual[:, i * part : (i + 1) * part].astype(F32)
        for ref in group:
            total = total + ref[...].astype(F32)
        squares = squares + jnp.sum(total * total, axis=-1, keepdims=True)
        width = outs[0].shape[1]
        for j in range(part // width):
            mixed[i * (part // width) + j] = total[:, j * width : (j + 1) * width]
    scale = lax.rsqrt(squares / (2 * part) + 1e-06)
    for k, out in enumerate(outs):
        out[...] = (mixed[meta[k]] * scale).astype(out.dtype)


def place_kernel(meta, *refs):
    out = refs[-1]
    for k, piece in enumerate(refs[:-1]):
        share = piece.shape[0]
        out[pl.ds(pl.multiple_of(meta[k] * share, share), share), :] = piece[...]


def anywhere(count):
    return [pl.BlockSpec(memory_space=pltpu.HBM)] * count


def in_vmem(count):
    return [pl.BlockSpec(memory_space=pltpu.VMEM)] * count


def small_call(kernel, name, meta, operands, outs, scratch=(), flops=0, limit=VMEM_SMALL):
    return pl.pallas_call(
        kernel,
        out_shape=outs,
        grid_spec=pltpu.PrefetchScalarGridSpec(
            num_scalar_prefetch=1,
            grid=(),
            in_specs=in_vmem(len(operands)),
            out_specs=tuple(in_vmem(len(outs))) if isinstance(outs, tuple) else in_vmem(1)[0],
            scratch_shapes=list(scratch),
        ),
        compiler_params=pltpu.CompilerParams(vmem_limit_bytes=limit),
        cost_estimate=pl.CostEstimate(flops=flops, bytes_accessed=4 * 1024 * 1024, transcendentals=0),
        name=name,
    )(meta, *operands)


def permuted_plan(prompt_hidden, qkv_weight, out_weight, embed_table, response_ids, assignment):
    grp, ctx, head = lax.axis_index("grp"), lax.axis_index("ctx"), lax.axis_index("head")
    nctx, nhead = lax.axis_size("ctx"), lax.axis_size("head")
    core, chip = ctx % 2, ctx // 2
    to_sib, to_far = xor_pairs(nctx, 1), xor_pairs(nctx, 2)
    fetch = [(g * nctx + c, g * nctx + (c ^ (2 + g))) for g in range(2) for c in range(nctx)]
    ring = shift_pairs(nhead, 1)
    prompts, prompt_rows, block = prompt_hidden.shape
    depth = block // 2
    cols = qkv_weight.shape[2] // 2
    steps = response_ids.shape[0]
    resp_local = response_ids.shape[1] // nctx
    rows_local = steps * resp_local

    sib = lambda array: permute(array, "ctx", to_sib)
    up = lambda array: permute(array, "head", ring)
    swap = lambda array: permute(array, "grp", xor_pairs(2, 1))

    def lookup(ids):
        offset_ids = ids - ctx * embed_table.shape[0]
        return jnp.take(embed_table, jnp.clip(offset_ids, 0, embed_table.shape[0] - 1), axis=0)

    def by_core(looked):
        vocab_rows = embed_table.shape[0]
        offset_ids = response_ids - ctx * vocab_rows
        inside = (offset_ids >= 0) & (offset_ids < vocab_rows)
        looked = jnp.where(inside[:, :, None], looked, jnp.zeros((), BF16))
        looked = looked.reshape(steps, nctx // 2, 2, resp_local, block)
        kept = lax.dynamic_index_in_dim(looked, core, 2, keepdims=False)
        given = lax.dynamic_index_in_dim(looked, 1 - core, 2, keepdims=False)

        def halves(received):
            total = kept + received
            mine = lax.dynamic_index_in_dim(total, chip, 1, keepdims=False)
            given = lax.dynamic_index_in_dim(total, 1 - chip, 1, keepdims=False)
            return mine.reshape(rows_local, block), given.reshape(rows_local, block)

        return given, halves

    width = out_weight.shape[1]
    tie = lax.optimization_barrier

    def fetched(k, weight):
        return lax.dynamic_slice(weight, (k, 0, (core ^ grp) * cols), (1, block, cols))[0]

    def cross(array):
        return permute(array, ("grp", "ctx"), fetch)

    first_half, later_weight = tie((fetched(1, qkv_weight), qkv_weight))
    keys_x = cross(first_half)
    tokens = [prompt_hidden, up(prompt_hidden)]
    sib_tokens = [sib(prompt_hidden)]
    looked = lookup(response_ids)

    keys_x, tokens, sib_tokens, looked, next_half, later_weight = tie(
        (keys_x, tokens, sib_tokens, looked, fetched(2, later_weight), later_weight)
    )
    values_x = cross(next_half)
    keys_y = swap(keys_x)
    tokens.append(up(tokens[1]))
    sib_tokens.append(sib(tokens[1]))
    given, halves_of = by_core(looked)
    mine, given = halves_of(sib(given))
    sib_weight = sib(lax.dynamic_slice(later_weight, (0, 0, (1 - core) * cols), (3, block, cols)))

    values_x, keys_y, tokens, sib_tokens, mine, given, next_half, sib_weight = tie(
        (values_x, keys_y, tokens, sib_tokens, mine, given, fetched(0, later_weight), sib_weight)
    )
    query_x = cross(next_half)
    given = permute(given, "ctx", to_far)
    values_y = swap(values_x)
    tokens.append(up(tokens[2]))
    sib_tokens.append(sib(tokens[2]))
    embedded = mine + given
    out_half = lax.dynamic_slice(out_weight, (grp * depth, 0), (depth, width))

    query_x, values_y, tokens, sib_tokens, embedded, out_half = tie(
        (query_x, values_y, tokens, sib_tokens, embedded, out_half)
    )
    out_x = permute(out_half, "ctx", to_far)
    query_y = swap(query_x)
    e = [embedded] + [permute(embedded, "head", shift_pairs(nhead, k)) for k in range(1, nhead)]
    sib_tokens.append(sib(tokens[3]))

    places = []
    for k in range(nhead):
        place = ctx ^ ((head - k) % nhead)
        places.append(jnp.where(place < 2, place, place ^ grp))
    meta = jnp.stack(places + [head, core, grp]).astype(jnp.int32)
    at_core = nhead + 1

    def own_spec(k, wide):
        return pl.BlockSpec((1, block, wide), lambda n, m: (k, 0, m[at_core] * (cols // wide) + n))

    def sib_spec(k, wide):
        return pl.BlockSpec((1, block, wide), lambda n, m: (k, 0, n))

    def far_spec(wide):
        return pl.BlockSpec((block, wide), lambda n, m: (0, n))

    crossed = ((query_x, query_y), (keys_x, keys_y), (values_x, values_y))
    far_of = lambda k: crossed[k]
    nblocks = 2 * nhead
    heads_here = cols // DH
    chip_tokens = 2 * prompts * prompt_rows

    state_spec = pl.BlockSpec((prompts, 1, DH, DH), lambda n, m: (0, n, 0, 0))
    states, rounded = pl.pallas_call(
        functools.partial(state_kernel, nblocks),
        out_shape=(
            jax.ShapeDtypeStruct((prompts, heads_here, DH, DH), F32),
            jax.ShapeDtypeStruct((prompts, heads_here, DH, DH), BF16),
        ),
        grid_spec=pltpu.PrefetchScalarGridSpec(
            num_scalar_prefetch=1,
            grid=(heads_here,),
            in_specs=anywhere(nblocks)
            + [own_spec(1, DH), own_spec(2, DH), sib_spec(1, DH), sib_spec(2, DH)]
            + [far_spec(DH)] * 4,
            out_specs=(state_spec, state_spec),
            scratch_shapes=[
                pltpu.VMEM((chip_tokens, nhead * block), BF16),
                pltpu.SemaphoreType.DMA((prompts * nblocks,)),
            ],
        ),
        compiler_params=pltpu.CompilerParams(vmem_limit_bytes=VMEM_LIMIT),
        cost_estimate=pl.CostEstimate(
            flops=4 * chip_tokens * nhead * block * cols, bytes_accessed=16 * 1024 * 1024, transcendentals=0
        ),
        name="prompt_state",
    )(
        meta,
        *tokens,
        *sib_tokens,
        qkv_weight,
        qkv_weight,
        sib_weight,
        sib_weight,
        *far_of(1),
        *far_of(2),
    )

    states, rounded, out_x, query_y, query_x, e, out_own = tie(
        (states, rounded, out_x, query_y, query_x, e, out_weight)
    )
    out_y = swap(out_x)
    others = permute(rounded, "ctx", to_far)
    e = jnp.stack(e)
    sib_e = sib(e)

    chip_rows = 2 * rows_local
    share = rows_local // nhead
    wide = 2 * DH
    row_spec = pl.BlockSpec((chip_rows, wide), lambda n, m: (0, n))
    query, local, residual = pl.pallas_call(
        functools.partial(project_kernel, nhead, steps),
        out_shape=(
            jax.ShapeDtypeStruct((chip_rows, cols), BF16),
            jax.ShapeDtypeStruct((chip_rows, cols), F32),
            jax.ShapeDtypeStruct((share, nhead * block), BF16),
        ),
        grid_spec=pltpu.PrefetchScalarGridSpec(
            num_scalar_prefetch=1,
            grid=(cols // wide,),
            in_specs=anywhere(2)
            + [own_spec(k, wide) for k in range(3)]
            + [sib_spec(k, wide) for k in range(3)]
            + [far_spec(wide)] * 6,
            out_specs=(row_spec, row_spec, pl.BlockSpec((share, nhead * block), lambda n, m: (0, 0))),
            scratch_shapes=[
                pltpu.VMEM((chip_rows, nhead * block), BF16),
                pltpu.SemaphoreType.DMA((nblocks,)),
            ],
        ),
        compiler_params=pltpu.CompilerParams(vmem_limit_bytes=VMEM_LIMIT),
        cost_estimate=pl.CostEstimate(
            flops=6 * chip_rows * nhead * block * cols, bytes_accessed=14 * 1024 * 1024, transcendentals=0
        ),
        name="response_rows",
    )(
        meta,
        e,
        sib_e,
        *([qkv_weight] * 3),
        *([sib_weight] * 3),
        *far_of(0),
        *far_of(1),
        *far_of(2),
    )

    which = [
        jnp.tile(lax.dynamic_slice_in_dim(assignment, owner * resp_local, resp_local, 0), steps)
        for owner in (ctx, ctx ^ 1)
    ]
    heads_own, heads_sib = pl.pallas_call(
        attend_kernel,
        out_shape=(jax.ShapeDtypeStruct((rows_local, cols), BF16),) * 2,
        compiler_params=pltpu.CompilerParams(vmem_limit_bytes=VMEM_SMALL),
        name="attend",
    )(query, local, jnp.concatenate(which)[:, None], states, others)
    heads_sib = sib(heads_sib)
    out_sib = sib(out_own)

    ahead = [(head + k) % nhead for k in range(nhead)]
    out_meta = jnp.stack(ahead + [core, grp]).astype(jnp.int32)

    def spread(kernel, name, heads, operands, scratch):
        outs = (jax.ShapeDtypeStruct((share, 2 * width), F32),)
        outs += (jax.ShapeDtypeStruct((share, 2 * width), BF16),) * (nhead - 1)
        scratch = [*scratch, pltpu.VMEM((rows_local, 2 * width), F32)]
        flops = 4 * rows_local * block * width
        terms = small_call(kernel, name, out_meta, (*heads, *operands), outs, scratch, flops, VMEM_LIMIT)
        moved = {k: permute(terms[k], "head", shift_pairs(nhead, k)) for k in (2, 3, 1)}
        return [terms[0]] + [moved[k] for k in range(1, nhead)]

    near = spread(near_kernel, "near_terms", (heads_own, heads_sib), (out_weight, out_sib), [])
    heads_own, heads_sib, out_y = tie((heads_own, heads_sib, out_y, near[0]))[:3]
    diag_x = sib(out_x)
    far = spread(
        far_kernel,
        "far_terms",
        (heads_own, heads_sib),
        (out_x, out_y, diag_x, sib(out_y)),
        [pltpu.VMEM((2, rows_local, cols), BF16)],
    )
    norm_meta = [ctx ^ f for f in ahead]
    norm_meta = jnp.stack([jnp.where(j < 2, j, j ^ grp) for j in norm_meta]).astype(jnp.int32)
    normed = small_call(
        functools.partial(norm_kernel, nhead),
        "final_norm",
        norm_meta,
        (residual, *near, *far),
        (jax.ShapeDtypeStruct((share, width), BF16),) * nhead,
        [pltpu.VMEM((nhead, share, width), F32)],
    )
    pieces = [normed[0]] + [permute(normed[k], "head", shift_pairs(nhead, k)) for k in range(1, nhead)]
    behind = jnp.stack([(head - k) % nhead for k in range(nhead)]).astype(jnp.int32)
    result = small_call(
        place_kernel, "place", behind, pieces, jax.ShapeDtypeStruct((rows_local, width), BF16)
    )
    return result.reshape(steps, resp_local, width)


def on_device(prompt_hidden, qkv_weight, out_weight, embed_table, response_ids, assignment):
    nctx, nhead = lax.axis_size("ctx"), lax.axis_size("head")
    local_heads = qkv_weight.shape[2] // DH
    fits = (
        lax.axis_size("grp") == 2
        and nctx == 4
        and nhead == 4
        and prompt_hidden.shape[0] == 2
        and local_heads % 4 == 0
        and prompt_hidden.shape[1] % 16 == 0
        and (response_ids.shape[1] // nctx) % (16 * nhead // response_ids.shape[0]) == 0
        and (response_ids.shape[1] // nctx) % 16 == 0
    )
    plan = permuted_plan if fits else gathered_plan
    return plan(prompt_hidden, qkv_weight, out_weight, embed_table, response_ids, assignment)


def solution(mesh):
    return jax.shard_map(
        on_device,
        mesh=mesh,
        in_specs=(
            P("grp", "ctx", "head"),
            P(None, "ctx", "head"),
            P("head", "ctx"),
            P("ctx", "head"),
            P(None, "grp"),
            P("grp"),
        ),
        out_specs=P(None, ("grp", "ctx"), "head"),
        check_vma=False,
    )
```

```python
import functools

import jax
import jax.numpy as jnp
from jax import lax
from jax.experimental import pallas as pl
from jax.experimental.pallas import tpu as pltpu
from jax.sharding import PartitionSpec as P

DH = 128
F32 = jnp.float32
BF16 = jnp.bfloat16
VMEM_LIMIT = 56 * 1024 * 1024
VMEM_SMALL = 16 * 1024 * 1024


def rms_rows(values):
    return values * lax.rsqrt(jnp.mean(values * values, axis=-1, keepdims=True) + 1e-06)


def gathered_plan(prompt_hidden, qkv_weight, out_weight, embed_table, response_ids, assignment):
    local_cols = prompt_hidden.shape[2]
    prompt_rows = prompt_hidden.shape[1]
    head_size = DH
    local_heads = local_cols // head_size
    steps = response_ids.shape[0]
    resp_local = response_ids.shape[1] // lax.axis_size("ctx")
    ctx_index = lax.axis_index("ctx")
    full_rows = lax.all_gather(qkv_weight, "ctx", axis=1, tiled=True)
    kv_weight = jnp.concatenate([full_rows[1], full_rows[2]], axis=1)
    piece = lax.all_gather(prompt_hidden, "head", axis=2, tiled=True)
    flat_piece = piece.reshape(2 * prompt_rows, piece.shape[2])
    kv_local = jnp.dot(flat_piece, kv_weight, preferred_element_type=jnp.float32)
    kv_local = kv_local.astype(jnp.bfloat16).reshape(2, prompt_rows, 2, local_heads, head_size)
    partial_state = jnp.einsum(
        "pthd,pthe->phde", kv_local[:, :, 0], kv_local[:, :, 1], preferred_element_type=jnp.float32
    )
    state = lax.psum(partial_state.astype(jnp.bfloat16), "ctx").astype(jnp.float32)
    vocab_rows = embed_table.shape[0]
    offset_ids = response_ids - ctx_index * vocab_rows
    inside = (offset_ids >= 0) & (offset_ids < vocab_rows)
    looked = jnp.take(embed_table, jnp.clip(offset_ids, 0, vocab_rows - 1), axis=0)
    looked = jnp.where(inside[:, :, None], looked.astype(jnp.float32), 0.0)
    embedded_mine = lax.psum_scatter(
        looked.astype(jnp.bfloat16), "ctx", scatter_dimension=1, tiled=True
    )
    embedded = lax.all_gather(embedded_mine, "head", axis=2, tiled=True)
    normed = rms_rows(embedded.astype(jnp.float32)).astype(jnp.bfloat16)
    projected_qkv = jnp.einsum(
        "trd,kde->trke", normed, full_rows, preferred_element_type=jnp.float32
    ).astype(jnp.bfloat16)
    projected_qkv = projected_qkv.reshape(steps, resp_local, 3, local_heads, head_size)
    query = projected_qkv[:, :, 0]
    key = projected_qkv[:, :, 1]
    value = projected_qkv[:, :, 2]
    my_prompt = lax.dynamic_slice_in_dim(assignment, ctx_index * resp_local, resp_local, 0)
    query_f = query.astype(jnp.float32)
    both = jnp.einsum("trhd,phde->ptrhe", query_f, state, precision=lax.Precision.HIGHEST)
    chosen = jnp.where((my_prompt == 0)[None, :, None, None], both[0], both[1])
    scores = jnp.einsum("trhd,srhd->rhts", query, key, preferred_element_type=jnp.float32)
    later = jnp.arange(steps)[:, None] >= jnp.arange(steps)[None, :]
    scores = jnp.where(later[None, None], scores, 0.0).astype(jnp.bfloat16)
    local = jnp.einsum("rhts,srhd->trhd", scores, value, preferred_element_type=jnp.float32)
    head_out = rms_rows(chosen + local).astype(jnp.bfloat16).reshape(steps, resp_local, local_cols)
    terms = jnp.einsum(
        "trd,de->tre",
        head_out,
        lax.all_gather(out_weight, "ctx", axis=1, tiled=True),
        preferred_element_type=jnp.float32,
    )
    width = terms.shape[2]
    mine = lax.psum_scatter(
        terms.astype(jnp.bfloat16), "head", scatter_dimension=2, tiled=True
    ).astype(jnp.float32)
    mixed = embedded_mine.astype(jnp.float32) + mine
    squares = lax.psum(jnp.sum(mixed * mixed, axis=-1), "head")
    result = mixed * lax.rsqrt(squares[:, :, None] / width + 1e-06)
    return result.astype(jnp.bfloat16)


def permute(array, axis, pairs):
    return lax.ppermute(array, axis, pairs)


def xor_pairs(count, mask):
    return [(i, i ^ mask) for i in range(count)]


def shift_pairs(count, by):
    return [(i, (i + by) % count) for i in range(count)]


def fetch_rows(meta, blocks, parts, held, sems):
    count = len(blocks) // parts
    block = held.shape[1] // count
    copies = []
    for part in range(parts):
        for k in range(count):
            rows = blocks[part * count + k].shape[0]
            at = pl.multiple_of(meta[k] * block, block)
            copies.append(
                pltpu.make_async_copy(
                    blocks[part * count + k],
                    held.at[pl.ds(part * rows, rows), pl.ds(at, block)],
                    sems.at[len(copies)],
                )
            )
    for copy in copies:
        copy.start()
    for copy in copies:
        copy.wait()


def held_dot(held, weights):
    total, at = None, 0
    for weight in weights:
        term = jnp.dot(held[:, at : at + weight.shape[0]], weight, preferred_element_type=F32)
        total = term if total is None else total + term
        at += weight.shape[0]
    return total


def state_kernel(nblocks, meta, *refs):
    blocks, refs = refs[:nblocks], refs[nblocks:]
    key_own, value_own, key_sib, value_sib = refs[:4]
    key_far, value_far = refs[4:6], refs[6:8]
    out, rounded, held, sems = refs[8:]
    prompts = out.shape[0]
    half = nblocks // 2

    @pl.when(pl.program_id(0) == 0)
    def _():
        parts = [blocks[s * half + k].at[p] for p in range(prompts) for s in range(2) for k in range(half)]
        fetch_rows(meta, parts, 2 * prompts, held, sems)

    keys = [key_own[0], key_sib[0]] + [ref[...] for ref in key_far]
    values = [value_own[0], value_sib[0]] + [ref[...] for ref in value_far]
    parts = [jnp.concatenate(pair, axis=1) for pair in zip(keys, values)]
    both = held_dot(held, parts).astype(BF16)
    tokens = both.shape[0] // prompts
    for p in range(prompts):
        rows = both[p * tokens : (p + 1) * tokens]
        state = lax.dot_general(
            rows[:, :DH], rows[:, DH:], (((0,), (0,)), ((), ())), preferred_element_type=F32
        )
        out[p, 0] = state
        rounded[p, 0] = state.astype(BF16)


def project_kernel(nhead, steps, meta, *refs):
    mine, other, refs = refs[:nhead], refs[nhead : 2 * nhead], refs[2 * nhead :]
    own, sib = refs[:3], refs[3:6]
    far = refs[6:8], refs[8:10], refs[10:12]
    query_out, local_out, residual, held = refs[12:]
    rows, block = held.shape[1:]
    features = nhead * block

    @pl.when(pl.program_id(0) == 0)
    def _():
        for k in range(nhead):
            held[meta[k], : rows // 2] = mine[k][...]
            held[meta[k], rows // 2 :] = other[k][...]
        share = residual.shape[0]
        at = pl.multiple_of(meta[nhead] * share, share)
        for j in range(nhead):
            residual[:, j * block : (j + 1) * block] = held[j, pl.ds(at, share), :]

    blocks = [held[j] for j in range(nhead)]

    squares = jnp.zeros((rows, 1), F32)
    for part in blocks:
        part = part.astype(F32)
        squares += jnp.sum(part * part, axis=-1, keepdims=True)
    scale = lax.rsqrt(squares / features + 1e-06)

    def projected(i):
        total = None
        for part, weight in zip(blocks, (own[i][0], sib[i][0], far[i][0][...], far[i][1][...])):
            term = jnp.dot(part, weight, preferred_element_type=F32)
            total = term if total is None else total + term
        return (total * scale).astype(BF16)

    query, key, value = (projected(i) for i in range(3))
    query_out[...] = query
    query, key, value = query.astype(F32), key.astype(F32), value.astype(F32)
    each = rows // 2 // steps
    for part in range(2):
        for s in range(steps):
            at_s = slice((part * steps + s) * each, (part * steps + s + 1) * each)
            for head in range(query.shape[1] // DH):
                cols = slice(head * DH, (head + 1) * DH)
                total = None
                for u in range(s + 1):
                    at_u = slice((part * steps + u) * each, (part * steps + u + 1) * each)
                    score = jnp.sum(query[at_s, cols] * key[at_u, cols], axis=-1, keepdims=True)
                    term = score.astype(BF16).astype(F32) * value[at_u, cols]
                    total = term if total is None else total + term
                local_out[at_s, cols] = total


def attend_kernel(query, local, chosen, states, others, out, given):
    second = chosen[...] != 0
    rows = out.shape[0]
    for head in range(states.shape[1]):
        cols = slice(head * DH, (head + 1) * DH)
        q = query[:, cols]
        both = []
        for p in range(2):
            state = states[p, head] + others[p, head].astype(F32)
            high = state.astype(BF16)
            low = (state - high.astype(F32)).astype(BF16)
            both.append(
                jnp.dot(q, high, preferred_element_type=F32) + jnp.dot(q, low, preferred_element_type=F32)
            )
        attended = jnp.where(second, both[1], both[0]) + local[:, cols]
        normed = rms_rows(attended).astype(BF16)
        out[:, cols] = normed[:rows]
        given[:, cols] = normed[rows:]


def share_out(meta, terms, outs):
    for k, out in enumerate(outs):
        share = out.shape[0]
        at = pl.multiple_of(meta[k] * share, share)
        out[...] = terms[pl.ds(at, share), :].astype(out.dtype)


def near_kernel(meta, heads_own, heads_sib, own, sib, *refs):
    outs, terms = refs[:-1], refs[-1]
    core = meta[len(outs)]
    half, width = heads_own.shape[1], own.shape[1]
    own_at = pl.multiple_of(core * half, half)
    sib_at = pl.multiple_of((1 - core) * half, half)
    for j, weight in enumerate((own, sib)):
        term = jnp.dot(heads_own[...], weight[pl.ds(own_at, half), :], preferred_element_type=F32)
        term += jnp.dot(heads_sib[...], weight[pl.ds(sib_at, half), :], preferred_element_type=F32)
        terms[:, j * width : (j + 1) * width] = term
    share_out(meta, terms, outs)


def far_kernel(meta, heads_own, heads_sib, far_x, far_y, diag_x, diag_y, *refs):
    outs, heads, terms = refs[:-2], refs[-2], refs[-1]
    core, group = meta[len(outs)], meta[len(outs) + 1]
    heads[core] = heads_own[...]
    heads[1 - core] = heads_sib[...]
    width = far_x.shape[1]
    for i, (first, second) in enumerate(((far_x, far_y), (diag_x, diag_y))):
        term = jnp.dot(heads[group], first[...], preferred_element_type=F32)
        term += jnp.dot(heads[1 - group], second[...], preferred_element_type=F32)
        at = pl.multiple_of((i ^ group) * width, width)
        terms[:, pl.ds(at, width)] = term
    share_out(meta, terms, outs)


def norm_kernel(nhead, meta, residual, *refs):
    near, far, outs, mixed = refs[:nhead], refs[nhead : 2 * nhead], refs[2 * nhead : 3 * nhead], refs[-1]
    part = near[0].shape[1]
    squares = 0.0
    for i, group in enumerate((near, far)):
        total = residual[:, i * part : (i + 1) * part].astype(F32)
        for ref in group:
            total = total + ref[...].astype(F32)
        squares = squares + jnp.sum(total * total, axis=-1, keepdims=True)
        width = outs[0].shape[1]
        for j in range(part // width):
            mixed[i * (part // width) + j] = total[:, j * width : (j + 1) * width]
    scale = lax.rsqrt(squares / (2 * part) + 1e-06)
    for k, out in enumerate(outs):
        out[...] = (mixed[meta[k]] * scale).astype(out.dtype)


def place_kernel(meta, *refs):
    out = refs[-1]
    for k, piece in enumerate(refs[:-1]):
        share = piece.shape[0]
        out[pl.ds(pl.multiple_of(meta[k] * share, share), share), :] = piece[...]


def anywhere(count):
    return [pl.BlockSpec(memory_space=pltpu.HBM)] * count


def in_vmem(count):
    return [pl.BlockSpec(memory_space=pltpu.VMEM)] * count


def small_call(kernel, name, meta, operands, outs, scratch=(), flops=0, limit=VMEM_SMALL):
    return pl.pallas_call(
        kernel,
        out_shape=outs,
        grid_spec=pltpu.PrefetchScalarGridSpec(
            num_scalar_prefetch=1,
            grid=(),
            in_specs=in_vmem(len(operands)),
            out_specs=tuple(in_vmem(len(outs))) if isinstance(outs, tuple) else in_vmem(1)[0],
            scratch_shapes=list(scratch),
        ),
        compiler_params=pltpu.CompilerParams(vmem_limit_bytes=limit),
        cost_estimate=pl.CostEstimate(flops=flops, bytes_accessed=4 * 1024 * 1024, transcendentals=0),
        name=name,
    )(meta, *operands)


def permuted_plan(prompt_hidden, qkv_weight, out_weight, embed_table, response_ids, assignment):
    grp, ctx, head = lax.axis_index("grp"), lax.axis_index("ctx"), lax.axis_index("head")
    nctx, nhead = lax.axis_size("ctx"), lax.axis_size("head")
    core, chip = ctx % 2, ctx // 2
    to_sib, to_far = xor_pairs(nctx, 1), xor_pairs(nctx, 2)
    fetch = [(g * nctx + c, g * nctx + (c ^ (2 + g))) for g in range(2) for c in range(nctx)]
    ring = shift_pairs(nhead, 1)
    prompts, prompt_rows, block = prompt_hidden.shape
    depth = block // 2
    cols = qkv_weight.shape[2] // 2
    steps = response_ids.shape[0]
    resp_local = response_ids.shape[1] // nctx
    rows_local = steps * resp_local

    sib = lambda array: permute(array, "ctx", to_sib)
    up = lambda array: permute(array, "head", ring)
    swap = lambda array: permute(array, "grp", xor_pairs(2, 1))

    def lookup(ids):
        offset_ids = ids - ctx * embed_table.shape[0]
        return jnp.take(embed_table, jnp.clip(offset_ids, 0, embed_table.shape[0] - 1), axis=0)

    def by_core(looked):
        vocab_rows = embed_table.shape[0]
        offset_ids = response_ids - ctx * vocab_rows
        inside = (offset_ids >= 0) & (offset_ids < vocab_rows)
        looked = jnp.where(inside[:, :, None], looked, jnp.zeros((), BF16))
        looked = looked.reshape(steps, nctx // 2, 2, resp_local, block)
        kept = lax.dynamic_index_in_dim(looked, core, 2, keepdims=False)
        given = lax.dynamic_index_in_dim(looked, 1 - core, 2, keepdims=False)

        def halves(received):
            total = kept + received
            mine = lax.dynamic_index_in_dim(total, chip, 1, keepdims=False)
            given = lax.dynamic_index_in_dim(total, 1 - chip, 1, keepdims=False)
            return mine.reshape(rows_local, block), given.reshape(rows_local, block)

        return given, halves

    width = out_weight.shape[1]
    tie = lax.optimization_barrier

    def fetched(k, weight):
        return lax.dynamic_slice(weight, (k, 0, (core ^ grp) * cols), (1, block, cols))[0]

    def cross(array):
        return permute(array, ("grp", "ctx"), fetch)

    places = []
    for k in range(nhead):
        place = ctx ^ ((head - k) % nhead)
        places.append(jnp.where(place < 2, place, place ^ grp))
    meta = jnp.stack(places + [head, core, grp]).astype(jnp.int32)
    at_core = nhead + 1

    ahead = [(head + k) % nhead for k in range(nhead)]
    out_meta = jnp.stack(ahead + [core, grp]).astype(jnp.int32)
    norm_meta = [ctx ^ f for f in ahead]
    norm_meta = jnp.stack([jnp.where(j < 2, j, j ^ grp) for j in norm_meta]).astype(jnp.int32)
    behind = jnp.stack([(head - k) % nhead for k in range(nhead)]).astype(jnp.int32)
    which = [
        jnp.tile(lax.dynamic_slice_in_dim(assignment, owner * resp_local, resp_local, 0), steps)
        for owner in (ctx, ctx ^ 1)
    ]
    chosen = jnp.concatenate(which)[:, None]

    first_half, later_weight, prompt_hidden = tie((fetched(1, qkv_weight), qkv_weight, prompt_hidden))
    tokens = [prompt_hidden, up(prompt_hidden)]
    keys_x = cross(first_half)
    sib_tokens = [sib(prompt_hidden)]
    sib_weight = sib(later_weight)
    next_half, ids, later_weight = tie((fetched(2, later_weight), response_ids, later_weight))
    given, halves_of = by_core(lookup(ids))

    metas = (meta, out_meta, norm_meta, behind, chosen)
    tokens, keys_x, sib_tokens, sib_weight, given, next_half, later_weight, metas = tie(
        (tokens, keys_x, sib_tokens, sib_weight, given, next_half, later_weight, metas)
    )
    meta, out_meta, norm_meta, behind, chosen = metas
    tokens.append(up(tokens[1]))
    values_x = cross(next_half)
    keys_y = swap(keys_x)
    sib_tokens.append(sib(tokens[1]))
    mine, given = halves_of(sib(given))
    given = permute(given, "ctx", to_far)

    tokens, values_x, keys_y, sib_tokens, mine, given, next_half = tie(
        (tokens, values_x, keys_y, sib_tokens, mine, given, fetched(0, later_weight))
    )
    tokens.append(up(tokens[2]))
    query_x = cross(next_half)
    values_y = swap(values_x)
    sib_tokens.append(sib(tokens[2]))
    embedded = mine + given
    sib_e = [sib(embedded)]
    out_half = lax.dynamic_slice(out_weight, (grp * depth, 0), (depth, width))

    tokens, query_x, values_y, sib_tokens, embedded, sib_e, out_half = tie(
        (tokens, query_x, values_y, sib_tokens, embedded, sib_e, out_half)
    )
    out_x = permute(out_half, "ctx", to_far)
    query_y = swap(query_x)
    e = [embedded] + [permute(embedded, "head", shift_pairs(nhead, k)) for k in range(1, nhead)]
    sib_tokens.append(sib(tokens[3]))

    def own_spec(k, wide):
        return pl.BlockSpec((1, block, wide), lambda n, m: (k, 0, m[at_core] * (cols // wide) + n))

    sib_spec = own_spec

    def far_spec(wide):
        return pl.BlockSpec((block, wide), lambda n, m: (0, n))

    crossed = ((query_x, query_y), (keys_x, keys_y), (values_x, values_y))
    far_of = lambda k: crossed[k]
    nblocks = 2 * nhead
    heads_here = cols // DH
    chip_tokens = 2 * prompts * prompt_rows

    state_spec = pl.BlockSpec((prompts, 1, DH, DH), lambda n, m: (0, n, 0, 0))
    states, rounded = pl.pallas_call(
        functools.partial(state_kernel, nblocks),
        out_shape=(
            jax.ShapeDtypeStruct((prompts, heads_here, DH, DH), F32),
            jax.ShapeDtypeStruct((prompts, heads_here, DH, DH), BF16),
        ),
        grid_spec=pltpu.PrefetchScalarGridSpec(
            num_scalar_prefetch=1,
            grid=(heads_here,),
            in_specs=anywhere(nblocks)
            + [own_spec(1, DH), own_spec(2, DH), sib_spec(1, DH), sib_spec(2, DH)]
            + [far_spec(DH)] * 4,
            out_specs=(state_spec, state_spec),
            scratch_shapes=[
                pltpu.VMEM((chip_tokens, nhead * block), BF16),
                pltpu.SemaphoreType.DMA((prompts * nblocks,)),
            ],
        ),
        compiler_params=pltpu.CompilerParams(vmem_limit_bytes=VMEM_LIMIT),
        cost_estimate=pl.CostEstimate(
            flops=4 * chip_tokens * nhead * block * cols, bytes_accessed=16 * 1024 * 1024, transcendentals=0
        ),
        name="prompt_state",
    )(
        meta,
        *tokens,
        *sib_tokens,
        qkv_weight,
        qkv_weight,
        sib_weight,
        sib_weight,
        *far_of(1),
        *far_of(2),
    )

    states, rounded, out_x, query_y, query_x, e, sib_e, out_own = tie(
        (states, rounded, out_x, query_y, query_x, e, sib_e, out_weight)
    )
    sib_e += [sib(array) for array in e[1:]]
    out_y = swap(out_x)
    others = permute(rounded, "ctx", to_far)

    chip_rows = 2 * rows_local
    share = rows_local // nhead
    wide = 2 * DH
    row_spec = pl.BlockSpec((chip_rows, wide), lambda n, m: (0, n))
    query, local, residual = pl.pallas_call(
        functools.partial(project_kernel, nhead, steps),
        out_shape=(
            jax.ShapeDtypeStruct((chip_rows, cols), BF16),
            jax.ShapeDtypeStruct((chip_rows, cols), F32),
            jax.ShapeDtypeStruct((share, nhead * block), BF16),
        ),
        grid_spec=pltpu.PrefetchScalarGridSpec(
            num_scalar_prefetch=1,
            grid=(cols // wide,),
            in_specs=[pl.BlockSpec((rows_local, block), lambda n, m: (0, 0))] * nblocks
            + [own_spec(k, wide) for k in range(3)]
            + [sib_spec(k, wide) for k in range(3)]
            + [far_spec(wide)] * 6,
            out_specs=(row_spec, row_spec, pl.BlockSpec((share, nhead * block), lambda n, m: (0, 0))),
            scratch_shapes=[pltpu.VMEM((nhead, chip_rows, block), BF16)],
        ),
        compiler_params=pltpu.CompilerParams(vmem_limit_bytes=VMEM_LIMIT),
        cost_estimate=pl.CostEstimate(
            flops=6 * chip_rows * nhead * block * cols, bytes_accessed=14 * 1024 * 1024, transcendentals=0
        ),
        name="response_rows",
    )(
        meta,
        *e,
        *sib_e,
        *([qkv_weight] * 3),
        *([sib_weight] * 3),
        *far_of(0),
        *far_of(1),
        *far_of(2),
    )

    heads_own, heads_sib = pl.pallas_call(
        attend_kernel,
        out_shape=(jax.ShapeDtypeStruct((rows_local, cols), BF16),) * 2,
        compiler_params=pltpu.CompilerParams(vmem_limit_bytes=VMEM_SMALL),
        name="attend",
    )(query, local, chosen, states, others)
    heads_sib = sib(heads_sib)
    out_sib = sib(out_own)

    def spread(kernel, name, heads, operands, scratch):
        outs = (jax.ShapeDtypeStruct((share, 2 * width), F32),)
        outs += (jax.ShapeDtypeStruct((share, 2 * width), BF16),) * (nhead - 1)
        scratch = [*scratch, pltpu.VMEM((rows_local, 2 * width), F32)]
        flops = 4 * rows_local * block * width
        terms = small_call(kernel, name, out_meta, (*heads, *operands), outs, scratch, flops)
        moved = {k: permute(terms[k], "head", shift_pairs(nhead, k)) for k in (2, 3, 1)}
        return [terms[0]] + [moved[k] for k in range(1, nhead)]

    near = spread(near_kernel, "near_terms", (heads_own, heads_sib), (out_weight, out_sib), [])
    heads_own, heads_sib, out_y = tie((heads_own, heads_sib, out_y, near[0]))[:3]
    diag_x = sib(out_x)
    far = spread(
        far_kernel,
        "far_terms",
        (heads_own, heads_sib),
        (out_x, out_y, diag_x, sib(out_y)),
        [pltpu.VMEM((2, rows_local, cols), BF16)],
    )
    normed = small_call(
        functools.partial(norm_kernel, nhead),
        "final_norm",
        norm_meta,
        (residual, *near, *far),
        (jax.ShapeDtypeStruct((share, width), BF16),) * nhead,
        [pltpu.VMEM((nhead, share, width), F32)],
    )
    pieces = [normed[0]] + [permute(normed[k], "head", shift_pairs(nhead, k)) for k in range(1, nhead)]
    result = small_call(
        place_kernel, "place", behind, pieces, jax.ShapeDtypeStruct((rows_local, width), BF16)
    )
    return result.reshape(steps, resp_local, width)


def on_device(prompt_hidden, qkv_weight, out_weight, embed_table, response_ids, assignment):
    nctx, nhead = lax.axis_size("ctx"), lax.axis_size("head")
    local_heads = qkv_weight.shape[2] // DH
    fits = (
        lax.axis_size("grp") == 2
        and nctx == 4
        and nhead == 4
        and prompt_hidden.shape[0] == 2
        and local_heads % 4 == 0
        and prompt_hidden.shape[1] % 16 == 0
        and (response_ids.shape[1] // nctx) % (16 * nhead // response_ids.shape[0]) == 0
        and (response_ids.shape[1] // nctx) % 16 == 0
    )
    plan = permuted_plan if fits else gathered_plan
    return plan(prompt_hidden, qkv_weight, out_weight, embed_table, response_ids, assignment)


def solution(mesh):
    return jax.shard_map(
        on_device,
        mesh=mesh,
        in_specs=(
            P("grp", "ctx", "head"),
            P(None, "ctx", "head"),
            P("head", "ctx"),
            P("ctx", "head"),
            P(None, "grp"),
            P("grp"),
        ),
        out_specs=P(None, ("grp", "ctx"), "head"),
        check_vma=False,
    )
```

```python
import functools

import jax
import jax.numpy as jnp
from jax import lax
from jax.experimental import pallas as pl
from jax.experimental.pallas import tpu as pltpu
from jax.sharding import PartitionSpec as P

DH = 128
F32 = jnp.float32
BF16 = jnp.bfloat16
VMEM_LIMIT = 56 * 1024 * 1024
VMEM_SMALL = 16 * 1024 * 1024


def rms_rows(values):
    return values * lax.rsqrt(jnp.mean(values * values, axis=-1, keepdims=True) + 1e-06)


def gathered_plan(prompt_hidden, qkv_weight, out_weight, embed_table, response_ids, assignment):
    local_cols = prompt_hidden.shape[2]
    prompt_rows = prompt_hidden.shape[1]
    head_size = DH
    local_heads = local_cols // head_size
    steps = response_ids.shape[0]
    resp_local = response_ids.shape[1] // lax.axis_size("ctx")
    ctx_index = lax.axis_index("ctx")
    full_rows = lax.all_gather(qkv_weight, "ctx", axis=1, tiled=True)
    kv_weight = jnp.concatenate([full_rows[1], full_rows[2]], axis=1)
    piece = lax.all_gather(prompt_hidden, "head", axis=2, tiled=True)
    flat_piece = piece.reshape(2 * prompt_rows, piece.shape[2])
    kv_local = jnp.dot(flat_piece, kv_weight, preferred_element_type=jnp.float32)
    kv_local = kv_local.astype(jnp.bfloat16).reshape(2, prompt_rows, 2, local_heads, head_size)
    partial_state = jnp.einsum(
        "pthd,pthe->phde", kv_local[:, :, 0], kv_local[:, :, 1], preferred_element_type=jnp.float32
    )
    state = lax.psum(partial_state.astype(jnp.bfloat16), "ctx").astype(jnp.float32)
    vocab_rows = embed_table.shape[0]
    offset_ids = response_ids - ctx_index * vocab_rows
    inside = (offset_ids >= 0) & (offset_ids < vocab_rows)
    looked = jnp.take(embed_table, jnp.clip(offset_ids, 0, vocab_rows - 1), axis=0)
    looked = jnp.where(inside[:, :, None], looked.astype(jnp.float32), 0.0)
    embedded_mine = lax.psum_scatter(
        looked.astype(jnp.bfloat16), "ctx", scatter_dimension=1, tiled=True
    )
    embedded = lax.all_gather(embedded_mine, "head", axis=2, tiled=True)
    normed = rms_rows(embedded.astype(jnp.float32)).astype(jnp.bfloat16)
    projected_qkv = jnp.einsum(
        "trd,kde->trke", normed, full_rows, preferred_element_type=jnp.float32
    ).astype(jnp.bfloat16)
    projected_qkv = projected_qkv.reshape(steps, resp_local, 3, local_heads, head_size)
    query = projected_qkv[:, :, 0]
    key = projected_qkv[:, :, 1]
    value = projected_qkv[:, :, 2]
    my_prompt = lax.dynamic_slice_in_dim(assignment, ctx_index * resp_local, resp_local, 0)
    query_f = query.astype(jnp.float32)
    both = jnp.einsum("trhd,phde->ptrhe", query_f, state, precision=lax.Precision.HIGHEST)
    chosen = jnp.where((my_prompt == 0)[None, :, None, None], both[0], both[1])
    scores = jnp.einsum("trhd,srhd->rhts", query, key, preferred_element_type=jnp.float32)
    later = jnp.arange(steps)[:, None] >= jnp.arange(steps)[None, :]
    scores = jnp.where(later[None, None], scores, 0.0).astype(jnp.bfloat16)
    local = jnp.einsum("rhts,srhd->trhd", scores, value, preferred_element_type=jnp.float32)
    head_out = rms_rows(chosen + local).astype(jnp.bfloat16).reshape(steps, resp_local, local_cols)
    terms = jnp.einsum(
        "trd,de->tre",
        head_out,
        lax.all_gather(out_weight, "ctx", axis=1, tiled=True),
        preferred_element_type=jnp.float32,
    )
    width = terms.shape[2]
    mine = lax.psum_scatter(
        terms.astype(jnp.bfloat16), "head", scatter_dimension=2, tiled=True
    ).astype(jnp.float32)
    mixed = embedded_mine.astype(jnp.float32) + mine
    squares = lax.psum(jnp.sum(mixed * mixed, axis=-1), "head")
    result = mixed * lax.rsqrt(squares[:, :, None] / width + 1e-06)
    return result.astype(jnp.bfloat16)


def permute(array, axis, pairs):
    return lax.ppermute(array, axis, pairs)


def xor_pairs(count, mask):
    return [(i, i ^ mask) for i in range(count)]


def shift_pairs(count, by):
    return [(i, (i + by) % count) for i in range(count)]


def fetch_rows(meta, blocks, parts, held, sems):
    count = len(blocks) // parts
    block = held.shape[1] // count
    copies = []
    for part in range(parts):
        for k in range(count):
            rows = blocks[part * count + k].shape[0]
            at = pl.multiple_of(meta[k] * block, block)
            copies.append(
                pltpu.make_async_copy(
                    blocks[part * count + k],
                    held.at[pl.ds(part * rows, rows), pl.ds(at, block)],
                    sems.at[len(copies)],
                )
            )
    for copy in copies:
        copy.start()
    for copy in copies:
        copy.wait()


def held_dot(held, weights):
    total, at = None, 0
    for weight in weights:
        term = jnp.dot(held[:, at : at + weight.shape[0]], weight, preferred_element_type=F32)
        total = term if total is None else total + term
        at += weight.shape[0]
    return total


def state_kernel(nblocks, meta, *refs):
    blocks, refs = refs[:nblocks], refs[nblocks:]
    key_own, value_own, key_sib, value_sib = refs[:4]
    key_far, value_far = refs[4:6], refs[6:8]
    out, rounded, held, sems = refs[8:]
    prompts = out.shape[0]
    half = nblocks // 2

    @pl.when(pl.program_id(0) == 0)
    def _():
        parts = [blocks[s * half + k].at[p] for p in range(prompts) for s in range(2) for k in range(half)]
        fetch_rows(meta, parts, 2 * prompts, held, sems)

    keys = [key_own[0], key_sib[0]] + [ref[...] for ref in key_far]
    values = [value_own[0], value_sib[0]] + [ref[...] for ref in value_far]
    parts = [jnp.concatenate(pair, axis=1) for pair in zip(keys, values)]
    both = held_dot(held, parts).astype(BF16)
    tokens = both.shape[0] // prompts
    for p in range(prompts):
        rows = both[p * tokens : (p + 1) * tokens]
        state = lax.dot_general(
            rows[:, :DH], rows[:, DH:], (((0,), (0,)), ((), ())), preferred_element_type=F32
        )
        out[p, 0] = state
        rounded[p, 0] = state.astype(BF16)


def project_kernel(nhead, steps, meta, *refs):
    mine, other, refs = refs[:nhead], refs[nhead : 2 * nhead], refs[2 * nhead :]
    own, sib = refs[:3], refs[3:6]
    far = refs[6:8], refs[8:10], refs[10:12]
    rows_out, residual, held = refs[12:]
    rows, block = held.shape[1:]
    features = nhead * block

    @pl.when(pl.program_id(0) == 0)
    def _():
        for k in range(nhead):
            held[meta[k], : rows // 2] = mine[k][...]
            held[meta[k], rows // 2 :] = other[k][...]
        share = residual.shape[0]
        at = pl.multiple_of(meta[nhead] * share, share)
        for j in range(nhead):
            residual[:, j * block : (j + 1) * block] = held[j, pl.ds(at, share), :]

    blocks = [held[j] for j in range(nhead)]

    squares = jnp.zeros((rows, 1), F32)
    for part in blocks:
        part = part.astype(F32)
        squares += jnp.sum(part * part, axis=-1, keepdims=True)
    scale = lax.rsqrt(squares / features + 1e-06)

    total = None
    for j, part in enumerate(blocks):
        each = [(own[i][0], sib[i][0], far[i][0][...], far[i][1][...])[j] for i in range(3)]
        term = jnp.dot(part, jnp.concatenate(each, axis=1), preferred_element_type=F32)
        total = term if total is None else total + term
    total = (total * scale).astype(BF16)
    wide = total.shape[1] // 3
    query, key, value = (total[:, i * wide : (i + 1) * wide] for i in range(3))
    width = query.shape[1]
    rows_out[:, :width] = query.astype(F32)
    query, key, value = query.astype(F32), key.astype(F32), value.astype(F32)
    each = rows // 2 // steps
    for part in range(2):
        for s in range(steps):
            at_s = slice((part * steps + s) * each, (part * steps + s + 1) * each)
            for head in range(query.shape[1] // DH):
                cols = slice(head * DH, (head + 1) * DH)
                total = None
                for u in range(s + 1):
                    at_u = slice((part * steps + u) * each, (part * steps + u + 1) * each)
                    score = jnp.sum(query[at_s, cols] * key[at_u, cols], axis=-1, keepdims=True)
                    term = score.astype(BF16).astype(F32) * value[at_u, cols]
                    total = term if total is None else total + term
                rows_out[at_s, width + head * DH : width + (head + 1) * DH] = total


def attend_kernel(wide, arrived, chosen, states, others, out, given):
    second = chosen[...] != 0
    rows = out.shape[0]
    for head in range(states.shape[1]):
        cols = slice(head * DH, (head + 1) * DH)
        at = 2 * wide * (head * DH // wide) + head * DH % wide
        q = arrived[:, at : at + DH].astype(BF16)
        both = []
        for p in range(2):
            state = states[p, head] + others[p, head].astype(F32)
            high = state.astype(BF16)
            low = (state - high.astype(F32)).astype(BF16)
            both.append(
                jnp.dot(q, high, preferred_element_type=F32) + jnp.dot(q, low, preferred_element_type=F32)
            )
        attended = jnp.where(second, both[1], both[0]) + arrived[:, at + wide : at + wide + DH]
        normed = rms_rows(attended).astype(BF16)
        out[:, cols] = normed[:rows]
        given[:, cols] = normed[rows:]


def share_out(meta, terms, outs):
    for k, out in enumerate(outs):
        share = out.shape[0]
        at = pl.multiple_of(meta[k] * share, share)
        out[...] = terms[pl.ds(at, share), :].astype(out.dtype)


def near_kernel(meta, heads_own, heads_sib, own, sib, *refs):
    outs, terms = refs[:-1], refs[-1]
    core = meta[len(outs)]
    half, width = heads_own.shape[1], own.shape[1]
    own_at = pl.multiple_of(core * half, half)
    sib_at = pl.multiple_of((1 - core) * half, half)
    for j, weight in enumerate((own, sib)):
        term = jnp.dot(heads_own[...], weight[pl.ds(own_at, half), :], preferred_element_type=F32)
        term += jnp.dot(heads_sib[...], weight[pl.ds(sib_at, half), :], preferred_element_type=F32)
        terms[:, j * width : (j + 1) * width] = term
    share_out(meta, terms, outs)


def far_kernel(meta, heads_own, heads_sib, far_x, far_y, diag_x, diag_y, *refs):
    outs, heads, terms = refs[:-2], refs[-2], refs[-1]
    core, group = meta[len(outs)], meta[len(outs) + 1]
    heads[core] = heads_own[...]
    heads[1 - core] = heads_sib[...]
    width = far_x.shape[1]
    for i, (first, second) in enumerate(((far_x, far_y), (diag_x, diag_y))):
        term = jnp.dot(heads[group], first[...], preferred_element_type=F32)
        term += jnp.dot(heads[1 - group], second[...], preferred_element_type=F32)
        at = pl.multiple_of((i ^ group) * width, width)
        terms[:, pl.ds(at, width)] = term
    share_out(meta, terms, outs)


def norm_kernel(nhead, meta, residual, *refs):
    near, far, outs, mixed = refs[:nhead], refs[nhead : 2 * nhead], refs[2 * nhead : 3 * nhead], refs[-1]
    part = near[0].shape[1]
    squares = 0.0
    for i, group in enumerate((near, far)):
        total = residual[:, i * part : (i + 1) * part].astype(F32)
        for ref in group:
            total = total + ref[...].astype(F32)
        squares = squares + jnp.sum(total * total, axis=-1, keepdims=True)
        width = outs[0].shape[1]
        for j in range(part // width):
            mixed[i * (part // width) + j] = total[:, j * width : (j + 1) * width]
    scale = lax.rsqrt(squares / (2 * part) + 1e-06)
    for k, out in enumerate(outs):
        out[...] = (mixed[meta[k]] * scale).astype(out.dtype)


def place_kernel(meta, *refs):
    out = refs[-1]
    for k, piece in enumerate(refs[:-1]):
        share = piece.shape[0]
        out[pl.ds(pl.multiple_of(meta[k] * share, share), share), :] = piece[...]


def anywhere(count):
    return [pl.BlockSpec(memory_space=pltpu.HBM)] * count


def in_vmem(count):
    return [pl.BlockSpec(memory_space=pltpu.VMEM)] * count


def small_call(kernel, name, meta, operands, outs, scratch=(), flops=0, limit=VMEM_SMALL):
    return pl.pallas_call(
        kernel,
        out_shape=outs,
        grid_spec=pltpu.PrefetchScalarGridSpec(
            num_scalar_prefetch=1,
            grid=(),
            in_specs=in_vmem(len(operands)),
            out_specs=tuple(in_vmem(len(outs))) if isinstance(outs, tuple) else in_vmem(1)[0],
            scratch_shapes=list(scratch),
        ),
        compiler_params=pltpu.CompilerParams(vmem_limit_bytes=limit),
        cost_estimate=pl.CostEstimate(flops=flops, bytes_accessed=4 * 1024 * 1024, transcendentals=0),
        name=name,
    )(meta, *operands)


def permuted_plan(prompt_hidden, qkv_weight, out_weight, embed_table, response_ids, assignment):
    grp, ctx, head = lax.axis_index("grp"), lax.axis_index("ctx"), lax.axis_index("head")
    nctx, nhead = lax.axis_size("ctx"), lax.axis_size("head")
    core, chip = ctx % 2, ctx // 2
    to_sib, to_far = xor_pairs(nctx, 1), xor_pairs(nctx, 2)
    fetch = [(g * nctx + c, g * nctx + (c ^ (2 + g))) for g in range(2) for c in range(nctx)]
    ring = shift_pairs(nhead, 1)
    prompts, prompt_rows, block = prompt_hidden.shape
    depth = block // 2
    cols = qkv_weight.shape[2] // 2
    steps = response_ids.shape[0]
    resp_local = response_ids.shape[1] // nctx
    rows_local = steps * resp_local

    sib = lambda array: permute(array, "ctx", to_sib)
    up = lambda array: permute(array, "head", ring)
    swap = lambda array: permute(array, "grp", xor_pairs(2, 1))

    def lookup(ids):
        offset_ids = ids - ctx * embed_table.shape[0]
        return jnp.take(embed_table, jnp.clip(offset_ids, 0, embed_table.shape[0] - 1), axis=0)

    def by_core(looked):
        vocab_rows = embed_table.shape[0]
        offset_ids = response_ids - ctx * vocab_rows
        inside = (offset_ids >= 0) & (offset_ids < vocab_rows)
        looked = jnp.where(inside[:, :, None], looked, jnp.zeros((), BF16))
        looked = looked.reshape(steps, nctx // 2, 2, resp_local, block)
        kept = lax.dynamic_index_in_dim(looked, core, 2, keepdims=False)
        given = lax.dynamic_index_in_dim(looked, 1 - core, 2, keepdims=False)

        def halves(received):
            total = kept + received
            mine = lax.dynamic_index_in_dim(total, chip, 1, keepdims=False)
            given = lax.dynamic_index_in_dim(total, 1 - chip, 1, keepdims=False)
            return mine.reshape(rows_local, block), given.reshape(rows_local, block)

        return given, halves

    width = out_weight.shape[1]
    tie = lax.optimization_barrier

    def fetched(k, weight):
        return lax.dynamic_slice(weight, (k, 0, (core ^ grp) * cols), (1, block, cols))[0]

    def cross(array):
        return permute(array, ("grp", "ctx"), fetch)

    places = []
    for k in range(nhead):
        place = ctx ^ ((head - k) % nhead)
        places.append(jnp.where(place < 2, place, place ^ grp))
    meta = jnp.stack(places + [head, core, grp]).astype(jnp.int32)
    at_core = nhead + 1

    ahead = [(head + k) % nhead for k in range(nhead)]
    out_meta = jnp.stack(ahead + [core, grp]).astype(jnp.int32)
    norm_meta = [ctx ^ f for f in ahead]
    norm_meta = jnp.stack([jnp.where(j < 2, j, j ^ grp) for j in norm_meta]).astype(jnp.int32)
    behind = jnp.stack([(head - k) % nhead for k in range(nhead)]).astype(jnp.int32)
    which = [
        jnp.tile(lax.dynamic_slice_in_dim(assignment, owner * resp_local, resp_local, 0), steps)
        for owner in (ctx, ctx ^ 1)
    ]
    chosen = jnp.concatenate(which)[:, None]

    first_half, later_weight, prompt_hidden = tie((fetched(1, qkv_weight), qkv_weight, prompt_hidden))
    tokens = [prompt_hidden, up(prompt_hidden)]
    keys_x = cross(first_half)
    sib_tokens = [sib(prompt_hidden)]
    sib_weight = sib(later_weight)
    out_sib = sib(out_weight)
    next_half, ids, later_weight = tie((fetched(2, later_weight), response_ids, later_weight))
    given, halves_of = by_core(lookup(ids))

    metas = (meta, out_meta, norm_meta, behind, chosen)
    next_half, tokens, keys_x, sib_tokens, sib_weight, given, later_weight, metas, out_sib = tie(
        (next_half, tokens, keys_x, sib_tokens, sib_weight, given, later_weight, metas, out_sib)
    )
    meta, out_meta, norm_meta, behind, chosen = metas
    values_x = cross(next_half)
    tokens.append(up(tokens[1]))
    keys_y = swap(keys_x)
    sib_tokens.append(sib(tokens[1]))
    mine, given = halves_of(sib(given))
    given = permute(given, "ctx", to_far)

    values_x, tokens, keys_y, sib_tokens, mine, next_half = tie(
        (values_x, tokens, keys_y, sib_tokens, mine, fetched(0, later_weight))
    )
    passed_on, given = tie((tokens[2], given))
    tokens.append(up(tokens[2]))
    query_x = cross(next_half)
    values_y = swap(values_x)
    sib_tokens.append(sib(passed_on))
    embedded = mine + given
    sib_e = [sib(embedded)]
    out_half = lax.dynamic_slice(out_weight, (grp * depth, 0), (depth, width))

    tokens, query_x, values_y, sib_tokens, embedded, sib_e, out_half = tie(
        (tokens, query_x, values_y, sib_tokens, embedded, sib_e, out_half)
    )
    out_x = permute(out_half, "ctx", to_far)
    query_y = swap(query_x)
    e = [embedded] + [permute(embedded, "head", shift_pairs(nhead, k)) for k in range(1, nhead)]
    sib_tokens.append(sib(tokens[3]))

    def own_spec(k, wide):
        return pl.BlockSpec((1, block, wide), lambda n, m: (k, 0, m[at_core] * (cols // wide) + n))

    sib_spec = own_spec

    def far_spec(wide):
        return pl.BlockSpec((block, wide), lambda n, m: (0, n))

    crossed = ((query_x, query_y), (keys_x, keys_y), (values_x, values_y))
    far_of = lambda k: crossed[k]
    nblocks = 2 * nhead
    heads_here = cols // DH
    chip_tokens = 2 * prompts * prompt_rows

    state_spec = pl.BlockSpec((prompts, 1, DH, DH), lambda n, m: (0, n, 0, 0))
    states, rounded = pl.pallas_call(
        functools.partial(state_kernel, nblocks),
        out_shape=(
            jax.ShapeDtypeStruct((prompts, heads_here, DH, DH), F32),
            jax.ShapeDtypeStruct((prompts, heads_here, DH, DH), BF16),
        ),
        grid_spec=pltpu.PrefetchScalarGridSpec(
            num_scalar_prefetch=1,
            grid=(heads_here,),
            in_specs=anywhere(nblocks)
            + [own_spec(1, DH), own_spec(2, DH), sib_spec(1, DH), sib_spec(2, DH)]
            + [far_spec(DH)] * 4,
            out_specs=(state_spec, state_spec),
            scratch_shapes=[
                pltpu.VMEM((chip_tokens, nhead * block), BF16),
                pltpu.SemaphoreType.DMA((prompts * nblocks,)),
            ],
        ),
        compiler_params=pltpu.CompilerParams(vmem_limit_bytes=VMEM_LIMIT),
        cost_estimate=pl.CostEstimate(
            flops=4 * chip_tokens * nhead * block * cols, bytes_accessed=16 * 1024 * 1024, transcendentals=0
        ),
        name="prompt_state",
    )(
        meta,
        *tokens,
        *sib_tokens,
        qkv_weight,
        qkv_weight,
        sib_weight,
        sib_weight,
        *far_of(1),
        *far_of(2),
    )

    states, rounded, out_x, query_y, query_x, e, sib_e = tie(
        (states, rounded, out_x, query_y, query_x, e, sib_e)
    )
    sib_e += [sib(array) for array in e[1:]]
    out_y = swap(out_x)
    others = permute(rounded, "ctx", to_far)

    chip_rows = 2 * rows_local
    share = rows_local // nhead
    wide = 2 * DH
    row_spec = pl.BlockSpec((chip_rows, 2 * wide), lambda n, m: (0, n))
    rows_out, residual = pl.pallas_call(
        functools.partial(project_kernel, nhead, steps),
        out_shape=(
            jax.ShapeDtypeStruct((chip_rows, 2 * cols), F32),
            jax.ShapeDtypeStruct((share, nhead * block), BF16),
        ),
        grid_spec=pltpu.PrefetchScalarGridSpec(
            num_scalar_prefetch=1,
            grid=(cols // wide,),
            in_specs=[pl.BlockSpec((rows_local, block), lambda n, m: (0, 0))] * nblocks
            + [own_spec(k, wide) for k in range(3)]
            + [sib_spec(k, wide) for k in range(3)]
            + [far_spec(wide)] * 6,
            out_specs=(row_spec, pl.BlockSpec((share, nhead * block), lambda n, m: (0, 0))),
            scratch_shapes=[pltpu.VMEM((nhead, chip_rows, block), BF16)],
        ),
        compiler_params=pltpu.CompilerParams(vmem_limit_bytes=VMEM_LIMIT),
        cost_estimate=pl.CostEstimate(
            flops=6 * chip_rows * nhead * block * cols, bytes_accessed=14 * 1024 * 1024, transcendentals=0
        ),
        name="response_rows",
    )(
        meta,
        *e,
        *sib_e,
        *([qkv_weight] * 3),
        *([sib_weight] * 3),
        *far_of(0),
        *far_of(1),
        *far_of(2),
    )

    heads_own, heads_sib = pl.pallas_call(
        functools.partial(attend_kernel, wide),
        out_shape=(jax.ShapeDtypeStruct((rows_local, cols), BF16),) * 2,
        compiler_params=pltpu.CompilerParams(vmem_limit_bytes=VMEM_SMALL),
        name="attend",
    )(rows_out, chosen, states, others)
    heads_sib = sib(heads_sib)

    def spread(kernel, name, heads, operands, scratch):
        outs = (jax.ShapeDtypeStruct((share, 2 * width), F32),)
        outs += (jax.ShapeDtypeStruct((share, 2 * width), BF16),) * (nhead - 1)
        scratch = [*scratch, pltpu.VMEM((rows_local, 2 * width), F32)]
        flops = 4 * rows_local * block * width
        terms = small_call(kernel, name, out_meta, (*heads, *operands), outs, scratch, flops)
        moved = {k: permute(terms[k], "head", shift_pairs(nhead, k)) for k in (2, 3, 1)}
        return [terms[0]] + [moved[k] for k in range(1, nhead)]

    near = spread(near_kernel, "near_terms", (heads_own, heads_sib), (out_weight, out_sib), [])
    heads_own, heads_sib, out_y = tie((heads_own, heads_sib, out_y, near[1]))[:3]
    diag_x = sib(out_x)
    far = spread(
        far_kernel,
        "far_terms",
        (heads_own, heads_sib),
        (out_x, out_y, diag_x, sib(out_y)),
        [pltpu.VMEM((2, rows_local, cols), BF16)],
    )
    normed = small_call(
        functools.partial(norm_kernel, nhead),
        "final_norm",
        norm_meta,
        (residual, *near, *far),
        (jax.ShapeDtypeStruct((share, width), BF16),) * nhead,
        [pltpu.VMEM((nhead, share, width), F32)],
    )
    pieces = [normed[0]] + [permute(normed[k], "head", shift_pairs(nhead, k)) for k in range(1, nhead)]
    result = small_call(
        place_kernel, "place", behind, pieces, jax.ShapeDtypeStruct((rows_local, width), BF16)
    )
    return result.reshape(steps, resp_local, width)


def on_device(prompt_hidden, qkv_weight, out_weight, embed_table, response_ids, assignment):
    nctx, nhead = lax.axis_size("ctx"), lax.axis_size("head")
    local_heads = qkv_weight.shape[2] // DH
    fits = (
        lax.axis_size("grp") == 2
        and nctx == 4
        and nhead == 4
        and prompt_hidden.shape[0] == 2
        and local_heads % 4 == 0
        and prompt_hidden.shape[1] % 16 == 0
        and (response_ids.shape[1] // nctx) % (16 * nhead // response_ids.shape[0]) == 0
        and (response_ids.shape[1] // nctx) % 16 == 0
    )
    plan = permuted_plan if fits else gathered_plan
    return plan(prompt_hidden, qkv_weight, out_weight, embed_table, response_ids, assignment)


def solution(mesh):
    return jax.shard_map(
        on_device,
        mesh=mesh,
        in_specs=(
            P("grp", "ctx", "head"),
            P(None, "ctx", "head"),
            P("head", "ctx"),
            P("ctx", "head"),
            P(None, "grp"),
            P("grp"),
        ),
        out_specs=P(None, ("grp", "ctx"), "head"),
        check_vma=False,
    )
```

```python
import functools

import jax
import jax.numpy as jnp
from jax import lax
from jax.experimental import pallas as pl
from jax.experimental.pallas import tpu as pltpu
from jax.sharding import PartitionSpec as P

DH = 128
F32 = jnp.float32
BF16 = jnp.bfloat16
VMEM_LIMIT = 56 * 1024 * 1024
VMEM_SMALL = 16 * 1024 * 1024


def rms_rows(values):
    return values * lax.rsqrt(jnp.mean(values * values, axis=-1, keepdims=True) + 1e-06)


def gathered_plan(prompt_hidden, qkv_weight, out_weight, embed_table, response_ids, assignment):
    local_cols = prompt_hidden.shape[2]
    prompt_rows = prompt_hidden.shape[1]
    head_size = DH
    local_heads = local_cols // head_size
    steps = response_ids.shape[0]
    resp_local = response_ids.shape[1] // lax.axis_size("ctx")
    ctx_index = lax.axis_index("ctx")
    full_rows = lax.all_gather(qkv_weight, "ctx", axis=1, tiled=True)
    kv_weight = jnp.concatenate([full_rows[1], full_rows[2]], axis=1)
    piece = lax.all_gather(prompt_hidden, "head", axis=2, tiled=True)
    flat_piece = piece.reshape(2 * prompt_rows, piece.shape[2])
    kv_local = jnp.dot(flat_piece, kv_weight, preferred_element_type=jnp.float32)
    kv_local = kv_local.astype(jnp.bfloat16).reshape(2, prompt_rows, 2, local_heads, head_size)
    partial_state = jnp.einsum(
        "pthd,pthe->phde", kv_local[:, :, 0], kv_local[:, :, 1], preferred_element_type=jnp.float32
    )
    state = lax.psum(partial_state.astype(jnp.bfloat16), "ctx").astype(jnp.float32)
    vocab_rows = embed_table.shape[0]
    offset_ids = response_ids - ctx_index * vocab_rows
    inside = (offset_ids >= 0) & (offset_ids < vocab_rows)
    looked = jnp.take(embed_table, jnp.clip(offset_ids, 0, vocab_rows - 1), axis=0)
    looked = jnp.where(inside[:, :, None], looked.astype(jnp.float32), 0.0)
    embedded_mine = lax.psum_scatter(
        looked.astype(jnp.bfloat16), "ctx", scatter_dimension=1, tiled=True
    )
    embedded = lax.all_gather(embedded_mine, "head", axis=2, tiled=True)
    normed = rms_rows(embedded.astype(jnp.float32)).astype(jnp.bfloat16)
    projected_qkv = jnp.einsum(
        "trd,kde->trke", normed, full_rows, preferred_element_type=jnp.float32
    ).astype(jnp.bfloat16)
    projected_qkv = projected_qkv.reshape(steps, resp_local, 3, local_heads, head_size)
    query = projected_qkv[:, :, 0]
    key = projected_qkv[:, :, 1]
    value = projected_qkv[:, :, 2]
    my_prompt = lax.dynamic_slice_in_dim(assignment, ctx_index * resp_local, resp_local, 0)
    query_f = query.astype(jnp.float32)
    both = jnp.einsum("trhd,phde->ptrhe", query_f, state, precision=lax.Precision.HIGHEST)
    chosen = jnp.where((my_prompt == 0)[None, :, None, None], both[0], both[1])
    scores = jnp.einsum("trhd,srhd->rhts", query, key, preferred_element_type=jnp.float32)
    later = jnp.arange(steps)[:, None] >= jnp.arange(steps)[None, :]
    scores = jnp.where(later[None, None], scores, 0.0).astype(jnp.bfloat16)
    local = jnp.einsum("rhts,srhd->trhd", scores, value, preferred_element_type=jnp.float32)
    head_out = rms_rows(chosen + local).astype(jnp.bfloat16).reshape(steps, resp_local, local_cols)
    terms = jnp.einsum(
        "trd,de->tre",
        head_out,
        lax.all_gather(out_weight, "ctx", axis=1, tiled=True),
        preferred_element_type=jnp.float32,
    )
    width = terms.shape[2]
    mine = lax.psum_scatter(
        terms.astype(jnp.bfloat16), "head", scatter_dimension=2, tiled=True
    ).astype(jnp.float32)
    mixed = embedded_mine.astype(jnp.float32) + mine
    squares = lax.psum(jnp.sum(mixed * mixed, axis=-1), "head")
    result = mixed * lax.rsqrt(squares[:, :, None] / width + 1e-06)
    return result.astype(jnp.bfloat16)


def permute(array, axis, pairs):
    return lax.ppermute(array, axis, pairs)


def xor_pairs(count, mask):
    return [(i, i ^ mask) for i in range(count)]


def shift_pairs(count, by):
    return [(i, (i + by) % count) for i in range(count)]


def fetch_rows(meta, blocks, parts, held, sems):
    count = len(blocks) // parts
    block = held.shape[1] // count
    copies = []
    for part in range(parts):
        for k in range(count):
            rows = blocks[part * count + k].shape[0]
            at = pl.multiple_of(meta[k] * block, block)
            copies.append(
                pltpu.make_async_copy(
                    blocks[part * count + k],
                    held.at[pl.ds(part * rows, rows), pl.ds(at, block)],
                    sems.at[len(copies)],
                )
            )
    for copy in copies:
        copy.start()
    for copy in copies:
        copy.wait()


def held_dot(held, weights):
    total, at = None, 0
    for weight in weights:
        term = jnp.dot(held[:, at : at + weight.shape[0]], weight, preferred_element_type=F32)
        total = term if total is None else total + term
        at += weight.shape[0]
    return total


def state_kernel(nblocks, meta, *refs):
    blocks, refs = refs[:nblocks], refs[nblocks:]
    key_own, value_own, key_sib, value_sib = refs[:4]
    key_far, value_far = refs[4:6], refs[6:8]
    out, rounded, held, sems = refs[8:]
    prompts = out.shape[0]
    half = nblocks // 2

    @pl.when(pl.program_id(0) == 0)
    def _():
        parts = [blocks[s * half + k].at[p] for p in range(prompts) for s in range(2) for k in range(half)]
        fetch_rows(meta, parts, 2 * prompts, held, sems)

    keys = [key_own[0], key_sib[0]] + [ref[...] for ref in key_far]
    values = [value_own[0], value_sib[0]] + [ref[...] for ref in value_far]
    parts = [jnp.concatenate(pair, axis=1) for pair in zip(keys, values)]
    both = held_dot(held, parts).astype(BF16)
    tokens = both.shape[0] // prompts
    for p in range(prompts):
        rows = both[p * tokens : (p + 1) * tokens]
        state = lax.dot_general(
            rows[:, :DH], rows[:, DH:], (((0,), (0,)), ((), ())), preferred_element_type=F32
        )
        out[p, 0] = state
        rounded[p, 0] = state.astype(BF16)


def project_kernel(nhead, steps, meta, *refs):
    mine, other, refs = refs[:nhead], refs[nhead : 2 * nhead], refs[2 * nhead :]
    own, sib = refs[:3], refs[3:6]
    far = refs[6:8], refs[8:10], refs[10:12]
    rows_out, residual, held = refs[12:]
    rows, block = held.shape[1:]
    features = nhead * block

    @pl.when(pl.program_id(0) == 0)
    def _():
        for k in range(nhead):
            held[meta[k], : rows // 2] = mine[k][...]
            held[meta[k], rows // 2 :] = other[k][...]
        share = residual.shape[0]
        at = pl.multiple_of(meta[nhead] * share, share)
        for j in range(nhead):
            residual[:, j * block : (j + 1) * block] = held[j, pl.ds(at, share), :]

    blocks = [held[j] for j in range(nhead)]

    squares = jnp.zeros((rows, 1), F32)
    for part in blocks:
        part = part.astype(F32)
        squares += jnp.sum(part * part, axis=-1, keepdims=True)
    scale = lax.rsqrt(squares / features + 1e-06)

    total = None
    for j, part in enumerate(blocks):
        each = [(own[i][0], sib[i][0], far[i][0][...], far[i][1][...])[j] for i in range(3)]
        term = jnp.dot(part, jnp.concatenate(each, axis=1), preferred_element_type=F32)
        total = term if total is None else total + term
    total = (total * scale).astype(BF16)
    wide = total.shape[1] // 3
    query, key, value = (total[:, i * wide : (i + 1) * wide] for i in range(3))
    width = query.shape[1]
    rows_out[:, :width] = query.astype(F32)
    query, key, value = query.astype(F32), key.astype(F32), value.astype(F32)
    each = rows // 2 // steps
    for part in range(2):
        for s in range(steps):
            at_s = slice((part * steps + s) * each, (part * steps + s + 1) * each)
            for head in range(query.shape[1] // DH):
                cols = slice(head * DH, (head + 1) * DH)
                total = None
                for u in range(s + 1):
                    at_u = slice((part * steps + u) * each, (part * steps + u + 1) * each)
                    score = jnp.sum(query[at_s, cols] * key[at_u, cols], axis=-1, keepdims=True)
                    term = score.astype(BF16).astype(F32) * value[at_u, cols]
                    total = term if total is None else total + term
                rows_out[at_s, width + head * DH : width + (head + 1) * DH] = total


def attend_kernel(wide, arrived, chosen, states, others, out, given):
    second = chosen[...] != 0
    rows = out.shape[0]
    for head in range(states.shape[1]):
        cols = slice(head * DH, (head + 1) * DH)
        at = 2 * wide * (head * DH // wide) + head * DH % wide
        q = arrived[:, at : at + DH].astype(BF16)
        both = []
        for p in range(2):
            state = states[p, head] + others[p, head].astype(F32)
            high = state.astype(BF16)
            low = (state - high.astype(F32)).astype(BF16)
            both.append(
                jnp.dot(q, high, preferred_element_type=F32) + jnp.dot(q, low, preferred_element_type=F32)
            )
        attended = jnp.where(second, both[1], both[0]) + arrived[:, at + wide : at + wide + DH]
        normed = rms_rows(attended).astype(BF16)
        out[:, cols] = normed[:rows]
        given[:, cols] = normed[rows:]


def share_out(meta, terms, outs):
    for k, out in enumerate(outs):
        share = out.shape[0]
        at = pl.multiple_of(meta[k] * share, share)
        out[...] = terms[pl.ds(at, share), :].astype(out.dtype)


def near_kernel(meta, heads_own, heads_sib, own, sib, *refs):
    outs, terms = refs[:-1], refs[-1]
    core = meta[len(outs)]
    half, width = heads_own.shape[1], own.shape[1]
    own_at = pl.multiple_of(core * half, half)
    sib_at = pl.multiple_of((1 - core) * half, half)
    for j, weight in enumerate((own, sib)):
        term = jnp.dot(heads_own[...], weight[pl.ds(own_at, half), :], preferred_element_type=F32)
        term += jnp.dot(heads_sib[...], weight[pl.ds(sib_at, half), :], preferred_element_type=F32)
        terms[:, j * width : (j + 1) * width] = term
    share_out(meta, terms, outs)


def far_kernel(meta, heads_own, heads_sib, far_x, far_y, diag_x, diag_y, *refs):
    outs, heads, terms = refs[:-2], refs[-2], refs[-1]
    core, group = meta[len(outs)], meta[len(outs) + 1]
    heads[core] = heads_own[...]
    heads[1 - core] = heads_sib[...]
    width = far_x.shape[1]
    for i, (first, second) in enumerate(((far_x, far_y), (diag_x, diag_y))):
        term = jnp.dot(heads[group], first[...], preferred_element_type=F32)
        term += jnp.dot(heads[1 - group], second[...], preferred_element_type=F32)
        at = pl.multiple_of((i ^ group) * width, width)
        terms[:, pl.ds(at, width)] = term
    share_out(meta, terms, outs)


def norm_kernel(nhead, meta, residual, *refs):
    near, far, outs, mixed = refs[:nhead], refs[nhead : 2 * nhead], refs[2 * nhead : 3 * nhead], refs[-1]
    part = near[0].shape[1]
    squares = 0.0
    for i, group in enumerate((near, far)):
        total = residual[:, i * part : (i + 1) * part].astype(F32)
        for ref in group:
            total = total + ref[...].astype(F32)
        squares = squares + jnp.sum(total * total, axis=-1, keepdims=True)
        width = outs[0].shape[1]
        for j in range(part // width):
            mixed[i * (part // width) + j] = total[:, j * width : (j + 1) * width]
    scale = lax.rsqrt(squares / (2 * part) + 1e-06)
    for k, out in enumerate(outs):
        out[...] = (mixed[meta[k]] * scale).astype(out.dtype)


def place_kernel(meta, *refs):
    out = refs[-1]
    for k, piece in enumerate(refs[:-1]):
        share = piece.shape[0]
        out[pl.ds(pl.multiple_of(meta[k] * share, share), share), :] = piece[...]


def anywhere(count):
    return [pl.BlockSpec(memory_space=pltpu.HBM)] * count


def in_vmem(count):
    return [pl.BlockSpec(memory_space=pltpu.VMEM)] * count


def small_call(kernel, name, meta, operands, outs, scratch=(), flops=0, limit=VMEM_SMALL):
    return pl.pallas_call(
        kernel,
        out_shape=outs,
        grid_spec=pltpu.PrefetchScalarGridSpec(
            num_scalar_prefetch=1,
            grid=(),
            in_specs=in_vmem(len(operands)),
            out_specs=tuple(in_vmem(len(outs))) if isinstance(outs, tuple) else in_vmem(1)[0],
            scratch_shapes=list(scratch),
        ),
        compiler_params=pltpu.CompilerParams(vmem_limit_bytes=limit),
        cost_estimate=pl.CostEstimate(flops=flops, bytes_accessed=4 * 1024 * 1024, transcendentals=0),
        name=name,
    )(meta, *operands)


def permuted_plan(prompt_hidden, qkv_weight, out_weight, embed_table, response_ids, assignment):
    grp, ctx, head = lax.axis_index("grp"), lax.axis_index("ctx"), lax.axis_index("head")
    nctx, nhead = lax.axis_size("ctx"), lax.axis_size("head")
    core, chip = ctx % 2, ctx // 2
    to_sib, to_far = xor_pairs(nctx, 1), xor_pairs(nctx, 2)
    fetch = [(g * nctx + c, g * nctx + (c ^ (2 + g))) for g in range(2) for c in range(nctx)]
    ring = shift_pairs(nhead, 1)
    prompts, prompt_rows, block = prompt_hidden.shape
    depth = block // 2
    cols = qkv_weight.shape[2] // 2
    steps = response_ids.shape[0]
    resp_local = response_ids.shape[1] // nctx
    rows_local = steps * resp_local

    sib = lambda array: permute(array, "ctx", to_sib)
    up = lambda array: permute(array, "head", ring)
    swap = lambda array: permute(array, "grp", xor_pairs(2, 1))

    def lookup(ids):
        offset_ids = ids - ctx * embed_table.shape[0]
        return jnp.take(embed_table, jnp.clip(offset_ids, 0, embed_table.shape[0] - 1), axis=0)

    def by_core(looked):
        vocab_rows = embed_table.shape[0]
        offset_ids = response_ids - ctx * vocab_rows
        inside = (offset_ids >= 0) & (offset_ids < vocab_rows)
        looked = jnp.where(inside[:, :, None], looked, jnp.zeros((), BF16))
        looked = looked.reshape(steps, nctx // 2, 2, resp_local, block)
        kept = lax.dynamic_index_in_dim(looked, core, 2, keepdims=False)
        given = lax.dynamic_index_in_dim(looked, 1 - core, 2, keepdims=False)

        def halves(received):
            total = kept + received
            mine = lax.dynamic_index_in_dim(total, chip, 1, keepdims=False)
            given = lax.dynamic_index_in_dim(total, 1 - chip, 1, keepdims=False)
            return mine.reshape(rows_local, block), given.reshape(rows_local, block)

        return given, halves

    width = out_weight.shape[1]
    tie = lax.optimization_barrier

    def fetched(k, weight):
        return lax.dynamic_slice(weight, (k, 0, (core ^ grp) * cols), (1, block, cols))[0]

    def cross(array):
        return permute(array, ("grp", "ctx"), fetch)

    places = []
    for k in range(nhead):
        place = ctx ^ ((head - k) % nhead)
        places.append(jnp.where(place < 2, place, place ^ grp))
    meta = jnp.stack(places + [head, core, grp]).astype(jnp.int32)
    at_core = nhead + 1

    ahead = [(head + k) % nhead for k in range(nhead)]
    out_meta = jnp.stack(ahead + [core, grp]).astype(jnp.int32)
    norm_meta = [ctx ^ f for f in ahead]
    norm_meta = jnp.stack([jnp.where(j < 2, j, j ^ grp) for j in norm_meta]).astype(jnp.int32)
    behind = jnp.stack([(head - k) % nhead for k in range(nhead)]).astype(jnp.int32)
    which = [
        jnp.tile(lax.dynamic_slice_in_dim(assignment, owner * resp_local, resp_local, 0), steps)
        for owner in (ctx, ctx ^ 1)
    ]
    chosen = jnp.concatenate(which)[:, None]

    first_half, later_weight, prompt_hidden = tie((fetched(1, qkv_weight), qkv_weight, prompt_hidden))
    tokens = [prompt_hidden, up(prompt_hidden)]
    keys_x = cross(first_half)
    sib_tokens = [sib(prompt_hidden)]
    sib_weight = sib(later_weight)
    out_sib = sib(out_weight)
    next_half, ids, later_weight = tie((fetched(2, later_weight), response_ids, later_weight))
    given, halves_of = by_core(lookup(ids))

    metas = (meta, out_meta, norm_meta, behind, chosen)
    next_half, tokens, keys_x, sib_tokens, sib_weight, given, later_weight, metas, out_sib = tie(
        (next_half, tokens, keys_x, sib_tokens, sib_weight, given, later_weight, metas, out_sib)
    )
    meta, out_meta, norm_meta, behind, chosen = metas
    values_x = cross(next_half)
    tokens.append(up(tokens[1]))
    keys_y = swap(keys_x)
    sib_tokens.append(sib(tokens[1]))
    mine, given = halves_of(sib(given))
    given = permute(given, "ctx", to_far)

    values_x, tokens, keys_y, sib_tokens, mine, next_half = tie(
        (values_x, tokens, keys_y, sib_tokens, mine, fetched(0, later_weight))
    )
    passed_on, given = tie((tokens[2], given))
    tokens.append(up(tokens[2]))
    query_x = cross(next_half)
    values_y = swap(values_x)
    sib_tokens.append(sib(passed_on))
    embedded = mine + given
    sib_e = [sib(embedded)]
    out_half = lax.dynamic_slice(out_weight, (grp * depth, 0), (depth, width))

    tokens, query_x, values_y, sib_tokens, embedded, sib_e, out_half = tie(
        (tokens, query_x, values_y, sib_tokens, embedded, sib_e, out_half)
    )
    out_x = permute(out_half, "ctx", to_far)
    query_y = swap(query_x)
    e = [embedded] + [permute(embedded, "head", shift_pairs(nhead, k)) for k in range(1, nhead)]
    sib_tokens.append(sib(tokens[3]))

    def own_spec(k, wide):
        return pl.BlockSpec((1, block, wide), lambda n, m: (k, 0, m[at_core] * (cols // wide) + n))

    sib_spec = own_spec

    def far_spec(wide):
        return pl.BlockSpec((block, wide), lambda n, m: (0, n))

    crossed = ((query_x, query_y), (keys_x, keys_y), (values_x, values_y))
    far_of = lambda k: crossed[k]
    nblocks = 2 * nhead
    heads_here = cols // DH
    chip_tokens = 2 * prompts * prompt_rows

    state_spec = pl.BlockSpec((prompts, 1, DH, DH), lambda n, m: (0, n, 0, 0))
    states, rounded = pl.pallas_call(
        functools.partial(state_kernel, nblocks),
        out_shape=(
            jax.ShapeDtypeStruct((prompts, heads_here, DH, DH), F32),
            jax.ShapeDtypeStruct((prompts, heads_here, DH, DH), BF16),
        ),
        grid_spec=pltpu.PrefetchScalarGridSpec(
            num_scalar_prefetch=1,
            grid=(heads_here,),
            in_specs=anywhere(nblocks)
            + [own_spec(1, DH), own_spec(2, DH), sib_spec(1, DH), sib_spec(2, DH)]
            + [far_spec(DH)] * 4,
            out_specs=(state_spec, state_spec),
            scratch_shapes=[
                pltpu.VMEM((chip_tokens, nhead * block), BF16),
                pltpu.SemaphoreType.DMA((prompts * nblocks,)),
            ],
        ),
        compiler_params=pltpu.CompilerParams(vmem_limit_bytes=VMEM_LIMIT),
        cost_estimate=pl.CostEstimate(
            flops=4 * chip_tokens * nhead * block * cols, bytes_accessed=16 * 1024 * 1024, transcendentals=0
        ),
        name="prompt_state",
    )(
        meta,
        *tokens,
        *sib_tokens,
        qkv_weight,
        qkv_weight,
        sib_weight,
        sib_weight,
        *far_of(1),
        *far_of(2),
    )

    states, rounded, e, sib_e = tie((states, rounded, e, sib_e))
    sib_e += [sib(array) for array in e[1:]]
    states, rounded, out_x, query_y, query_x = tie((states, rounded, out_x, query_y, query_x))
    out_y = swap(out_x)
    others = permute(rounded, "ctx", to_far)

    chip_rows = 2 * rows_local
    share = rows_local // nhead
    wide = 2 * DH
    row_spec = pl.BlockSpec((chip_rows, 2 * wide), lambda n, m: (0, n))
    rows_out, residual = pl.pallas_call(
        functools.partial(project_kernel, nhead, steps),
        out_shape=(
            jax.ShapeDtypeStruct((chip_rows, 2 * cols), F32),
            jax.ShapeDtypeStruct((share, nhead * block), BF16),
        ),
        grid_spec=pltpu.PrefetchScalarGridSpec(
            num_scalar_prefetch=1,
            grid=(cols // wide,),
            in_specs=[pl.BlockSpec((rows_local, block), lambda n, m: (0, 0))] * nblocks
            + [own_spec(k, wide) for k in range(3)]
            + [sib_spec(k, wide) for k in range(3)]
            + [far_spec(wide)] * 6,
            out_specs=(row_spec, pl.BlockSpec((share, nhead * block), lambda n, m: (0, 0))),
            scratch_shapes=[pltpu.VMEM((nhead, chip_rows, block), BF16)],
        ),
        compiler_params=pltpu.CompilerParams(vmem_limit_bytes=VMEM_LIMIT),
        cost_estimate=pl.CostEstimate(
            flops=6 * chip_rows * nhead * block * cols, bytes_accessed=14 * 1024 * 1024, transcendentals=0
        ),
        name="response_rows",
    )(
        meta,
        *e,
        *sib_e,
        *([qkv_weight] * 3),
        *([sib_weight] * 3),
        *far_of(0),
        *far_of(1),
        *far_of(2),
    )

    heads_own, heads_sib = pl.pallas_call(
        functools.partial(attend_kernel, wide),
        out_shape=(jax.ShapeDtypeStruct((rows_local, cols), BF16),) * 2,
        compiler_params=pltpu.CompilerParams(vmem_limit_bytes=VMEM_SMALL),
        name="attend",
    )(rows_out, chosen, states, others)
    heads_sib = sib(heads_sib)

    def spread(kernel, name, heads, operands, scratch):
        outs = (jax.ShapeDtypeStruct((share, 2 * width), F32),)
        outs += (jax.ShapeDtypeStruct((share, 2 * width), BF16),) * (nhead - 1)
        scratch = [*scratch, pltpu.VMEM((rows_local, 2 * width), F32)]
        flops = 4 * rows_local * block * width
        terms = small_call(kernel, name, out_meta, (*heads, *operands), outs, scratch, flops)
        moved = {k: permute(terms[k], "head", shift_pairs(nhead, k)) for k in (2, 3, 1)}
        return [terms[0]] + [moved[k] for k in range(1, nhead)]

    near = spread(near_kernel, "near_terms", (heads_own, heads_sib), (out_weight, out_sib), [])
    heads_own, heads_sib, out_y = tie((heads_own, heads_sib, out_y, near[2]))[:3]
    diag_x = sib(out_x)
    far = spread(
        far_kernel,
        "far_terms",
        (heads_own, heads_sib),
        (out_x, out_y, diag_x, sib(out_y)),
        [pltpu.VMEM((2, rows_local, cols), BF16)],
    )
    normed = small_call(
        functools.partial(norm_kernel, nhead),
        "final_norm",
        norm_meta,
        (residual, *near, *far),
        (jax.ShapeDtypeStruct((share, width), BF16),) * nhead,
        [pltpu.VMEM((nhead, share, width), F32)],
    )
    pieces = [normed[0]] + [permute(normed[k], "head", shift_pairs(nhead, k)) for k in range(1, nhead)]
    result = small_call(
        place_kernel, "place", behind, pieces, jax.ShapeDtypeStruct((rows_local, width), BF16)
    )
    return result.reshape(steps, resp_local, width)


def on_device(prompt_hidden, qkv_weight, out_weight, embed_table, response_ids, assignment):
    nctx, nhead = lax.axis_size("ctx"), lax.axis_size("head")
    local_heads = qkv_weight.shape[2] // DH
    fits = (
        lax.axis_size("grp") == 2
        and nctx == 4
        and nhead == 4
        and prompt_hidden.shape[0] == 2
        and local_heads % 4 == 0
        and prompt_hidden.shape[1] % 16 == 0
        and (response_ids.shape[1] // nctx) % (16 * nhead // response_ids.shape[0]) == 0
        and (response_ids.shape[1] // nctx) % 16 == 0
    )
    plan = permuted_plan if fits else gathered_plan
    return plan(prompt_hidden, qkv_weight, out_weight, embed_table, response_ids, assignment)


def solution(mesh):
    return jax.shard_map(
        on_device,
        mesh=mesh,
        in_specs=(
            P("grp", "ctx", "head"),
            P(None, "ctx", "head"),
            P("head", "ctx"),
            P("ctx", "head"),
            P(None, "grp"),
            P("grp"),
        ),
        out_specs=P(None, ("grp", "ctx"), "head"),
        check_vma=False,
    )
```

```python
import functools

import jax
import jax.numpy as jnp
from jax import lax
from jax.experimental import pallas as pl
from jax.experimental.pallas import tpu as pltpu
from jax.sharding import PartitionSpec as P

DH = 128
F32 = jnp.float32
BF16 = jnp.bfloat16
VMEM_LIMIT = 56 * 1024 * 1024
VMEM_SMALL = 16 * 1024 * 1024


def rms_rows(values):
    return values * lax.rsqrt(jnp.mean(values * values, axis=-1, keepdims=True) + 1e-06)


def gathered_plan(prompt_hidden, qkv_weight, out_weight, embed_table, response_ids, assignment):
    local_cols = prompt_hidden.shape[2]
    prompt_rows = prompt_hidden.shape[1]
    head_size = DH
    local_heads = local_cols // head_size
    steps = response_ids.shape[0]
    resp_local = response_ids.shape[1] // lax.axis_size("ctx")
    ctx_index = lax.axis_index("ctx")
    full_rows = lax.all_gather(qkv_weight, "ctx", axis=1, tiled=True)
    kv_weight = jnp.concatenate([full_rows[1], full_rows[2]], axis=1)
    piece = lax.all_gather(prompt_hidden, "head", axis=2, tiled=True)
    flat_piece = piece.reshape(2 * prompt_rows, piece.shape[2])
    kv_local = jnp.dot(flat_piece, kv_weight, preferred_element_type=jnp.float32)
    kv_local = kv_local.astype(jnp.bfloat16).reshape(2, prompt_rows, 2, local_heads, head_size)
    partial_state = jnp.einsum(
        "pthd,pthe->phde", kv_local[:, :, 0], kv_local[:, :, 1], preferred_element_type=jnp.float32
    )
    state = lax.psum(partial_state.astype(jnp.bfloat16), "ctx").astype(jnp.float32)
    vocab_rows = embed_table.shape[0]
    offset_ids = response_ids - ctx_index * vocab_rows
    inside = (offset_ids >= 0) & (offset_ids < vocab_rows)
    looked = jnp.take(embed_table, jnp.clip(offset_ids, 0, vocab_rows - 1), axis=0)
    looked = jnp.where(inside[:, :, None], looked.astype(jnp.float32), 0.0)
    embedded_mine = lax.psum_scatter(
        looked.astype(jnp.bfloat16), "ctx", scatter_dimension=1, tiled=True
    )
    embedded = lax.all_gather(embedded_mine, "head", axis=2, tiled=True)
    normed = rms_rows(embedded.astype(jnp.float32)).astype(jnp.bfloat16)
    projected_qkv = jnp.einsum(
        "trd,kde->trke", normed, full_rows, preferred_element_type=jnp.float32
    ).astype(jnp.bfloat16)
    projected_qkv = projected_qkv.reshape(steps, resp_local, 3, local_heads, head_size)
    query = projected_qkv[:, :, 0]
    key = projected_qkv[:, :, 1]
    value = projected_qkv[:, :, 2]
    my_prompt = lax.dynamic_slice_in_dim(assignment, ctx_index * resp_local, resp_local, 0)
    query_f = query.astype(jnp.float32)
    both = jnp.einsum("trhd,phde->ptrhe", query_f, state, precision=lax.Precision.HIGHEST)
    chosen = jnp.where((my_prompt == 0)[None, :, None, None], both[0], both[1])
    scores = jnp.einsum("trhd,srhd->rhts", query, key, preferred_element_type=jnp.float32)
    later = jnp.arange(steps)[:, None] >= jnp.arange(steps)[None, :]
    scores = jnp.where(later[None, None], scores, 0.0).astype(jnp.bfloat16)
    local = jnp.einsum("rhts,srhd->trhd", scores, value, preferred_element_type=jnp.float32)
    head_out = rms_rows(chosen + local).astype(jnp.bfloat16).reshape(steps, resp_local, local_cols)
    terms = jnp.einsum(
        "trd,de->tre",
        head_out,
        lax.all_gather(out_weight, "ctx", axis=1, tiled=True),
        preferred_element_type=jnp.float32,
    )
    width = terms.shape[2]
    mine = lax.psum_scatter(
        terms.astype(jnp.bfloat16), "head", scatter_dimension=2, tiled=True
    ).astype(jnp.float32)
    mixed = embedded_mine.astype(jnp.float32) + mine
    squares = lax.psum(jnp.sum(mixed * mixed, axis=-1), "head")
    result = mixed * lax.rsqrt(squares[:, :, None] / width + 1e-06)
    return result.astype(jnp.bfloat16)


def permute(array, axis, pairs):
    return lax.ppermute(array, axis, pairs)


def xor_pairs(count, mask):
    return [(i, i ^ mask) for i in range(count)]


def shift_pairs(count, by):
    return [(i, (i + by) % count) for i in range(count)]


def fetch_rows(meta, blocks, parts, held, sems):
    count = len(blocks) // parts
    block = held.shape[1] // count
    copies = []
    for part in range(parts):
        for k in range(count):
            rows = blocks[part * count + k].shape[0]
            at = pl.multiple_of(meta[k] * block, block)
            copies.append(
                pltpu.make_async_copy(
                    blocks[part * count + k],
                    held.at[pl.ds(part * rows, rows), pl.ds(at, block)],
                    sems.at[len(copies)],
                )
            )
    for copy in copies:
        copy.start()
    for copy in copies:
        copy.wait()


def held_dot(held, weights):
    total, at = None, 0
    for weight in weights:
        term = jnp.dot(held[:, at : at + weight.shape[0]], weight, preferred_element_type=F32)
        total = term if total is None else total + term
        at += weight.shape[0]
    return total


def state_kernel(nblocks, meta, *refs):
    blocks, refs = refs[:nblocks], refs[nblocks:]
    key_own, value_own, key_sib, value_sib = refs[:4]
    key_far, value_far = refs[4:6], refs[6:8]
    out, rounded, held, sems = refs[8:]
    prompts = out.shape[0]
    half = nblocks // 2

    @pl.when(pl.program_id(0) == 0)
    def _():
        parts = [blocks[s * half + k].at[p] for p in range(prompts) for s in range(2) for k in range(half)]
        fetch_rows(meta, parts, 2 * prompts, held, sems)

    keys = [key_own[0], key_sib[0]] + [ref[...] for ref in key_far]
    values = [value_own[0], value_sib[0]] + [ref[...] for ref in value_far]
    parts = [jnp.concatenate(pair, axis=1) for pair in zip(keys, values)]
    both = held_dot(held, parts).astype(BF16)
    tokens = both.shape[0] // prompts
    for p in range(prompts):
        rows = both[p * tokens : (p + 1) * tokens]
        state = lax.dot_general(
            rows[:, :DH], rows[:, DH:], (((0,), (0,)), ((), ())), preferred_element_type=F32
        )
        out[p, 0] = state
        rounded[p, 0] = state.astype(BF16)


def project_kernel(nhead, steps, meta, *refs):
    mine, other, refs = refs[:nhead], refs[nhead : 2 * nhead], refs[2 * nhead :]
    own, sib = refs[:3], refs[3:6]
    far = refs[6:8], refs[8:10], refs[10:12]
    rows_out, residual, held = refs[12:]
    rows, block = held.shape[1:]
    features = nhead * block

    @pl.when(pl.program_id(0) == 0)
    def _():
        for k in range(nhead):
            held[meta[k], : rows // 2] = mine[k][...]
            held[meta[k], rows // 2 :] = other[k][...]
        share = residual.shape[0]
        at = pl.multiple_of(meta[nhead] * share, share)
        for j in range(nhead):
            residual[:, j * block : (j + 1) * block] = held[j, pl.ds(at, share), :]

    blocks = [held[j] for j in range(nhead)]

    squares = jnp.zeros((rows, 1), F32)
    for part in blocks:
        part = part.astype(F32)
        squares += jnp.sum(part * part, axis=-1, keepdims=True)
    scale = lax.rsqrt(squares / features + 1e-06)

    total = None
    for j, part in enumerate(blocks):
        each = [(own[i][0], sib[i][0], far[i][0][...], far[i][1][...])[j] for i in range(3)]
        term = jnp.dot(part, jnp.concatenate(each, axis=1), preferred_element_type=F32)
        total = term if total is None else total + term
    total = (total * scale).astype(BF16)
    wide = total.shape[1] // 3
    query, key, value = (total[:, i * wide : (i + 1) * wide] for i in range(3))
    width = query.shape[1]
    rows_out[:, :width] = query.astype(F32)
    query, key, value = query.astype(F32), key.astype(F32), value.astype(F32)
    each = rows // 2 // steps
    for part in range(2):
        for s in range(steps):
            at_s = slice((part * steps + s) * each, (part * steps + s + 1) * each)
            for head in range(query.shape[1] // DH):
                cols = slice(head * DH, (head + 1) * DH)
                total = None
                for u in range(s + 1):
                    at_u = slice((part * steps + u) * each, (part * steps + u + 1) * each)
                    score = jnp.sum(query[at_s, cols] * key[at_u, cols], axis=-1, keepdims=True)
                    term = score.astype(BF16).astype(F32) * value[at_u, cols]
                    total = term if total is None else total + term
                rows_out[at_s, width + head * DH : width + (head + 1) * DH] = total


def attend_kernel(wide, arrived, chosen, states, others, out, given):
    second = chosen[...] != 0
    rows = out.shape[0]
    for head in range(states.shape[1]):
        cols = slice(head * DH, (head + 1) * DH)
        at = 2 * wide * (head * DH // wide) + head * DH % wide
        q = arrived[:, at : at + DH].astype(BF16)
        both = []
        for p in range(2):
            state = states[p, head] + others[p, head].astype(F32)
            high = state.astype(BF16)
            low = (state - high.astype(F32)).astype(BF16)
            both.append(
                jnp.dot(q, high, preferred_element_type=F32) + jnp.dot(q, low, preferred_element_type=F32)
            )
        attended = jnp.where(second, both[1], both[0]) + arrived[:, at + wide : at + wide + DH]
        normed = rms_rows(attended).astype(BF16)
        out[:, cols] = normed[:rows]
        given[:, cols] = normed[rows:]


def share_out(meta, terms, outs):
    for k, out in enumerate(outs):
        share = out.shape[0]
        at = pl.multiple_of(meta[k] * share, share)
        out[...] = terms[pl.ds(at, share), :].astype(out.dtype)


def near_kernel(meta, heads_own, heads_sib, own, sib, *refs):
    outs, terms = refs[:-1], refs[-1]
    core = meta[len(outs)]
    half, width = heads_own.shape[1], own.shape[1]
    own_at = pl.multiple_of(core * half, half)
    sib_at = pl.multiple_of((1 - core) * half, half)
    for j, weight in enumerate((own, sib)):
        term = jnp.dot(heads_own[...], weight[pl.ds(own_at, half), :], preferred_element_type=F32)
        term += jnp.dot(heads_sib[...], weight[pl.ds(sib_at, half), :], preferred_element_type=F32)
        terms[:, j * width : (j + 1) * width] = term
    share_out(meta, terms, outs)


def far_kernel(meta, heads_own, heads_sib, far_x, far_y, diag_x, diag_y, *refs):
    outs, heads, terms = refs[:-2], refs[-2], refs[-1]
    core, group = meta[len(outs)], meta[len(outs) + 1]
    heads[core] = heads_own[...]
    heads[1 - core] = heads_sib[...]
    width = far_x.shape[1]
    for i, (first, second) in enumerate(((far_x, far_y), (diag_x, diag_y))):
        term = jnp.dot(heads[group], first[...], preferred_element_type=F32)
        term += jnp.dot(heads[1 - group], second[...], preferred_element_type=F32)
        at = pl.multiple_of((i ^ group) * width, width)
        terms[:, pl.ds(at, width)] = term
    share_out(meta, terms, outs)


def norm_kernel(nhead, meta, residual, *refs):
    near, far, outs, mixed = refs[:nhead], refs[nhead : 2 * nhead], refs[2 * nhead : 3 * nhead], refs[-1]
    part = near[0].shape[1]
    squares = 0.0
    for i, group in enumerate((near, far)):
        total = residual[:, i * part : (i + 1) * part].astype(F32)
        for ref in group:
            total = total + ref[...].astype(F32)
        squares = squares + jnp.sum(total * total, axis=-1, keepdims=True)
        width = outs[0].shape[1]
        for j in range(part // width):
            mixed[i * (part // width) + j] = total[:, j * width : (j + 1) * width]
    scale = lax.rsqrt(squares / (2 * part) + 1e-06)
    for k, out in enumerate(outs):
        out[...] = (mixed[meta[k]] * scale).astype(out.dtype)


def place_kernel(meta, *refs):
    out = refs[-1]
    for k, piece in enumerate(refs[:-1]):
        share = piece.shape[0]
        out[pl.ds(pl.multiple_of(meta[k] * share, share), share), :] = piece[...]


def anywhere(count):
    return [pl.BlockSpec(memory_space=pltpu.HBM)] * count


def in_vmem(count):
    return [pl.BlockSpec(memory_space=pltpu.VMEM)] * count


def small_call(kernel, name, meta, operands, outs, scratch=(), flops=0, limit=VMEM_SMALL):
    return pl.pallas_call(
        kernel,
        out_shape=outs,
        grid_spec=pltpu.PrefetchScalarGridSpec(
            num_scalar_prefetch=1,
            grid=(),
            in_specs=in_vmem(len(operands)),
            out_specs=tuple(in_vmem(len(outs))) if isinstance(outs, tuple) else in_vmem(1)[0],
            scratch_shapes=list(scratch),
        ),
        compiler_params=pltpu.CompilerParams(vmem_limit_bytes=limit),
        cost_estimate=pl.CostEstimate(flops=flops, bytes_accessed=4 * 1024 * 1024, transcendentals=0),
        name=name,
    )(meta, *operands)


def permuted_plan(prompt_hidden, qkv_weight, out_weight, embed_table, response_ids, assignment):
    grp, ctx, head = lax.axis_index("grp"), lax.axis_index("ctx"), lax.axis_index("head")
    nctx, nhead = lax.axis_size("ctx"), lax.axis_size("head")
    core, chip = ctx % 2, ctx // 2
    to_sib, to_far = xor_pairs(nctx, 1), xor_pairs(nctx, 2)
    fetch = [(g * nctx + c, g * nctx + (c ^ (2 + g))) for g in range(2) for c in range(nctx)]
    ring = shift_pairs(nhead, 1)
    prompts, prompt_rows, block = prompt_hidden.shape
    depth = block // 2
    cols = qkv_weight.shape[2] // 2
    steps = response_ids.shape[0]
    resp_local = response_ids.shape[1] // nctx
    rows_local = steps * resp_local

    sib = lambda array: permute(array, "ctx", to_sib)
    up = lambda array: permute(array, "head", ring)
    swap = lambda array: permute(array, "grp", xor_pairs(2, 1))

    def lookup(ids):
        offset_ids = ids - ctx * embed_table.shape[0]
        return jnp.take(embed_table, jnp.clip(offset_ids, 0, embed_table.shape[0] - 1), axis=0)

    def by_core(looked):
        vocab_rows = embed_table.shape[0]
        offset_ids = response_ids - ctx * vocab_rows
        inside = (offset_ids >= 0) & (offset_ids < vocab_rows)
        looked = jnp.where(inside[:, :, None], looked, jnp.zeros((), BF16))
        looked = looked.reshape(steps, nctx // 2, 2, resp_local, block)
        kept = lax.dynamic_index_in_dim(looked, core, 2, keepdims=False)
        given = lax.dynamic_index_in_dim(looked, 1 - core, 2, keepdims=False)

        def halves(received):
            total = kept + received
            mine = lax.dynamic_index_in_dim(total, chip, 1, keepdims=False)
            given = lax.dynamic_index_in_dim(total, 1 - chip, 1, keepdims=False)
            return mine.reshape(rows_local, block), given.reshape(rows_local, block)

        return given, halves

    width = out_weight.shape[1]
    tie = lax.optimization_barrier

    def fetched(k, weight):
        return lax.dynamic_slice(weight, (k, 0, (core ^ grp) * cols), (1, block, cols))[0]

    def cross(array):
        return permute(array, ("grp", "ctx"), fetch)

    places = []
    for k in range(nhead):
        place = ctx ^ ((head - k) % nhead)
        places.append(jnp.where(place < 2, place, place ^ grp))
    meta = jnp.stack(places + [head, core, grp]).astype(jnp.int32)
    at_core = nhead + 1

    ahead = [(head + k) % nhead for k in range(nhead)]
    out_meta = jnp.stack(ahead + [core, grp]).astype(jnp.int32)
    norm_meta = [ctx ^ f for f in ahead]
    norm_meta = jnp.stack([jnp.where(j < 2, j, j ^ grp) for j in norm_meta]).astype(jnp.int32)
    behind = jnp.stack([(head - k) % nhead for k in range(nhead)]).astype(jnp.int32)
    which = [
        jnp.tile(lax.dynamic_slice_in_dim(assignment, owner * resp_local, resp_local, 0), steps)
        for owner in (ctx, ctx ^ 1)
    ]
    chosen = jnp.concatenate(which)[:, None]

    first_half, later_weight, prompt_hidden = tie((fetched(1, qkv_weight), qkv_weight, prompt_hidden))
    tokens = [prompt_hidden, up(prompt_hidden)]
    keys_x = cross(first_half)
    sib_tokens = [sib(prompt_hidden)]
    sib_weight = sib(later_weight)
    out_sib = sib(out_weight)
    next_half, ids, later_weight = tie((fetched(2, later_weight), response_ids, later_weight))
    given, halves_of = by_core(lookup(ids))

    metas = (meta, out_meta, norm_meta, behind, chosen)
    query_half = fetched(0, later_weight)
    next_half, tokens, keys_x, sib_tokens, sib_weight, given, query_half, metas, out_sib = tie(
        (next_half, tokens, keys_x, sib_tokens, sib_weight, given, query_half, metas, out_sib)
    )
    meta, out_meta, norm_meta, behind, chosen = metas
    values_x = cross(next_half)
    tokens.append(up(tokens[1]))
    keys_y = swap(keys_x)
    sib_tokens.append(sib(tokens[1]))
    mine, given = halves_of(sib(given))
    given = permute(given, "ctx", to_far)

    query_x = cross(query_half)
    values_x, tokens, keys_y, sib_tokens, mine = tie((values_x, tokens, keys_y, sib_tokens, mine))
    tokens.append(up(tokens[2]))
    values_y = swap(values_x)
    sib_tokens.append(sib(tokens[2]))
    embedded = mine + given
    out_half = lax.dynamic_slice(out_weight, (grp * depth, 0), (depth, width))

    tokens, query_x, values_y, sib_tokens, embedded, out_half = tie(
        (tokens, query_x, values_y, sib_tokens, embedded, out_half)
    )
    out_x = permute(out_half, "ctx", to_far)
    query_y = swap(query_x)
    e = [embedded] + [permute(embedded, "head", shift_pairs(nhead, k)) for k in range(1, nhead)]
    sib_tokens.append(sib(tokens[3]))

    def own_spec(k, wide):
        return pl.BlockSpec((1, block, wide), lambda n, m: (k, 0, m[at_core] * (cols // wide) + n))

    sib_spec = own_spec

    def far_spec(wide):
        return pl.BlockSpec((block, wide), lambda n, m: (0, n))

    crossed = ((query_x, query_y), (keys_x, keys_y), (values_x, values_y))
    far_of = lambda k: crossed[k]
    nblocks = 2 * nhead
    heads_here = cols // DH
    chip_tokens = 2 * prompts * prompt_rows

    state_spec = pl.BlockSpec((prompts, 1, DH, DH), lambda n, m: (0, n, 0, 0))
    states, rounded = pl.pallas_call(
        functools.partial(state_kernel, nblocks),
        out_shape=(
            jax.ShapeDtypeStruct((prompts, heads_here, DH, DH), F32),
            jax.ShapeDtypeStruct((prompts, heads_here, DH, DH), BF16),
        ),
        grid_spec=pltpu.PrefetchScalarGridSpec(
            num_scalar_prefetch=1,
            grid=(heads_here,),
            in_specs=anywhere(nblocks)
            + [own_spec(1, DH), own_spec(2, DH), sib_spec(1, DH), sib_spec(2, DH)]
            + [far_spec(DH)] * 4,
            out_specs=(state_spec, state_spec),
            scratch_shapes=[
                pltpu.VMEM((chip_tokens, nhead * block), BF16),
                pltpu.SemaphoreType.DMA((prompts * nblocks,)),
            ],
        ),
        compiler_params=pltpu.CompilerParams(vmem_limit_bytes=VMEM_LIMIT),
        cost_estimate=pl.CostEstimate(
            flops=4 * chip_tokens * nhead * block * cols, bytes_accessed=16 * 1024 * 1024, transcendentals=0
        ),
        name="prompt_state",
    )(
        meta,
        *tokens,
        *sib_tokens,
        qkv_weight,
        qkv_weight,
        sib_weight,
        sib_weight,
        *far_of(1),
        *far_of(2),
    )

    states, rounded, e = tie((states, rounded, e))
    sib_e = [sib(array) for array in e]
    states, rounded, out_x, query_y, query_x = tie((states, rounded, out_x, query_y, query_x))
    out_y = swap(out_x)
    others = permute(rounded, "ctx", to_far)

    chip_rows = 2 * rows_local
    share = rows_local // nhead
    wide = 2 * DH
    row_spec = pl.BlockSpec((chip_rows, 2 * wide), lambda n, m: (0, n))
    rows_out, residual = pl.pallas_call(
        functools.partial(project_kernel, nhead, steps),
        out_shape=(
            jax.ShapeDtypeStruct((chip_rows, 2 * cols), F32),
            jax.ShapeDtypeStruct((share, nhead * block), BF16),
        ),
        grid_spec=pltpu.PrefetchScalarGridSpec(
            num_scalar_prefetch=1,
            grid=(cols // wide,),
            in_specs=[pl.BlockSpec((rows_local, block), lambda n, m: (0, 0))] * nblocks
            + [own_spec(k, wide) for k in range(3)]
            + [sib_spec(k, wide) for k in range(3)]
            + [far_spec(wide)] * 6,
            out_specs=(row_spec, pl.BlockSpec((share, nhead * block), lambda n, m: (0, 0))),
            scratch_shapes=[pltpu.VMEM((nhead, chip_rows, block), BF16)],
        ),
        compiler_params=pltpu.CompilerParams(vmem_limit_bytes=VMEM_LIMIT),
        cost_estimate=pl.CostEstimate(
            flops=6 * chip_rows * nhead * block * cols, bytes_accessed=14 * 1024 * 1024, transcendentals=0
        ),
        name="response_rows",
    )(
        meta,
        *e,
        *sib_e,
        *([qkv_weight] * 3),
        *([sib_weight] * 3),
        *far_of(0),
        *far_of(1),
        *far_of(2),
    )

    heads_own, heads_sib = pl.pallas_call(
        functools.partial(attend_kernel, wide),
        out_shape=(jax.ShapeDtypeStruct((rows_local, cols), BF16),) * 2,
        compiler_params=pltpu.CompilerParams(vmem_limit_bytes=VMEM_SMALL),
        name="attend",
    )(rows_out, chosen, states, others)
    heads_sib = sib(heads_sib)

    def spread(kernel, name, heads, operands, scratch):
        outs = (jax.ShapeDtypeStruct((share, 2 * width), F32),)
        outs += (jax.ShapeDtypeStruct((share, 2 * width), BF16),) * (nhead - 1)
        scratch = [*scratch, pltpu.VMEM((rows_local, 2 * width), F32)]
        flops = 4 * rows_local * block * width
        terms = small_call(kernel, name, out_meta, (*heads, *operands), outs, scratch, flops)
        moved = {k: permute(terms[k], "head", shift_pairs(nhead, k)) for k in (2, 3, 1)}
        return [terms[0]] + [moved[k] for k in range(1, nhead)]

    near = spread(near_kernel, "near_terms", (heads_own, heads_sib), (out_weight, out_sib), [])
    heads_own, heads_sib, out_y = tie((heads_own, heads_sib, out_y, near[2]))[:3]
    diag_x = sib(out_x)
    far = spread(
        far_kernel,
        "far_terms",
        (heads_own, heads_sib),
        (out_x, out_y, diag_x, sib(out_y)),
        [pltpu.VMEM((2, rows_local, cols), BF16)],
    )
    normed = small_call(
        functools.partial(norm_kernel, nhead),
        "final_norm",
        norm_meta,
        (residual, *near, *far),
        (jax.ShapeDtypeStruct((share, width), BF16),) * nhead,
        [pltpu.VMEM((nhead, share, width), F32)],
    )
    pieces = [normed[0]] + [permute(normed[k], "head", shift_pairs(nhead, k)) for k in range(1, nhead)]
    result = small_call(
        place_kernel, "place", behind, pieces, jax.ShapeDtypeStruct((rows_local, width), BF16)
    )
    return result.reshape(steps, resp_local, width)


def on_device(prompt_hidden, qkv_weight, out_weight, embed_table, response_ids, assignment):
    nctx, nhead = lax.axis_size("ctx"), lax.axis_size("head")
    local_heads = qkv_weight.shape[2] // DH
    fits = (
        lax.axis_size("grp") == 2
        and nctx == 4
        and nhead == 4
        and prompt_hidden.shape[0] == 2
        and local_heads % 4 == 0
        and prompt_hidden.shape[1] % 16 == 0
        and (response_ids.shape[1] // nctx) % (16 * nhead // response_ids.shape[0]) == 0
        and (response_ids.shape[1] // nctx) % 16 == 0
    )
    plan = permuted_plan if fits else gathered_plan
    return plan(prompt_hidden, qkv_weight, out_weight, embed_table, response_ids, assignment)


def solution(mesh):
    return jax.shard_map(
        on_device,
        mesh=mesh,
        in_specs=(
            P("grp", "ctx", "head"),
            P(None, "ctx", "head"),
            P("head", "ctx"),
            P("ctx", "head"),
            P(None, "grp"),
            P("grp"),
        ),
        out_specs=P(None, ("grp", "ctx"), "head"),
        check_vma=False,
    )
```

```python
import functools

import jax
import jax.numpy as jnp
from jax import lax
from jax.experimental import pallas as pl
from jax.experimental.pallas import tpu as pltpu
from jax.sharding import PartitionSpec as P

DH = 128
F32 = jnp.float32
BF16 = jnp.bfloat16
VMEM_LIMIT = 56 * 1024 * 1024
VMEM_SMALL = 16 * 1024 * 1024


def rms_rows(values):
    return values * lax.rsqrt(jnp.mean(values * values, axis=-1, keepdims=True) + 1e-06)


def gathered_plan(prompt_hidden, qkv_weight, out_weight, embed_table, response_ids, assignment):
    local_cols = prompt_hidden.shape[2]
    prompt_rows = prompt_hidden.shape[1]
    head_size = DH
    local_heads = local_cols // head_size
    steps = response_ids.shape[0]
    resp_local = response_ids.shape[1] // lax.axis_size("ctx")
    ctx_index = lax.axis_index("ctx")
    full_rows = lax.all_gather(qkv_weight, "ctx", axis=1, tiled=True)
    kv_weight = jnp.concatenate([full_rows[1], full_rows[2]], axis=1)
    piece = lax.all_gather(prompt_hidden, "head", axis=2, tiled=True)
    flat_piece = piece.reshape(2 * prompt_rows, piece.shape[2])
    kv_local = jnp.dot(flat_piece, kv_weight, preferred_element_type=jnp.float32)
    kv_local = kv_local.astype(jnp.bfloat16).reshape(2, prompt_rows, 2, local_heads, head_size)
    partial_state = jnp.einsum(
        "pthd,pthe->phde", kv_local[:, :, 0], kv_local[:, :, 1], preferred_element_type=jnp.float32
    )
    state = lax.psum(partial_state.astype(jnp.bfloat16), "ctx").astype(jnp.float32)
    vocab_rows = embed_table.shape[0]
    offset_ids = response_ids - ctx_index * vocab_rows
    inside = (offset_ids >= 0) & (offset_ids < vocab_rows)
    looked = jnp.take(embed_table, jnp.clip(offset_ids, 0, vocab_rows - 1), axis=0)
    looked = jnp.where(inside[:, :, None], looked.astype(jnp.float32), 0.0)
    embedded_mine = lax.psum_scatter(
        looked.astype(jnp.bfloat16), "ctx", scatter_dimension=1, tiled=True
    )
    embedded = lax.all_gather(embedded_mine, "head", axis=2, tiled=True)
    normed = rms_rows(embedded.astype(jnp.float32)).astype(jnp.bfloat16)
    projected_qkv = jnp.einsum(
        "trd,kde->trke", normed, full_rows, preferred_element_type=jnp.float32
    ).astype(jnp.bfloat16)
    projected_qkv = projected_qkv.reshape(steps, resp_local, 3, local_heads, head_size)
    query = projected_qkv[:, :, 0]
    key = projected_qkv[:, :, 1]
    value = projected_qkv[:, :, 2]
    my_prompt = lax.dynamic_slice_in_dim(assignment, ctx_index * resp_local, resp_local, 0)
    query_f = query.astype(jnp.float32)
    both = jnp.einsum("trhd,phde->ptrhe", query_f, state, precision=lax.Precision.HIGHEST)
    chosen = jnp.where((my_prompt == 0)[None, :, None, None], both[0], both[1])
    scores = jnp.einsum("trhd,srhd->rhts", query, key, preferred_element_type=jnp.float32)
    later = jnp.arange(steps)[:, None] >= jnp.arange(steps)[None, :]
    scores = jnp.where(later[None, None], scores, 0.0).astype(jnp.bfloat16)
    local = jnp.einsum("rhts,srhd->trhd", scores, value, preferred_element_type=jnp.float32)
    head_out = rms_rows(chosen + local).astype(jnp.bfloat16).reshape(steps, resp_local, local_cols)
    terms = jnp.einsum(
        "trd,de->tre",
        head_out,
        lax.all_gather(out_weight, "ctx", axis=1, tiled=True),
        preferred_element_type=jnp.float32,
    )
    width = terms.shape[2]
    mine = lax.psum_scatter(
        terms.astype(jnp.bfloat16), "head", scatter_dimension=2, tiled=True
    ).astype(jnp.float32)
    mixed = embedded_mine.astype(jnp.float32) + mine
    squares = lax.psum(jnp.sum(mixed * mixed, axis=-1), "head")
    result = mixed * lax.rsqrt(squares[:, :, None] / width + 1e-06)
    return result.astype(jnp.bfloat16)


def permute(array, axis, pairs):
    return lax.ppermute(array, axis, pairs)


def xor_pairs(count, mask):
    return [(i, i ^ mask) for i in range(count)]


def shift_pairs(count, by):
    return [(i, (i + by) % count) for i in range(count)]


def fetch_rows(meta, blocks, parts, held, sems):
    count = len(blocks) // parts
    block = held.shape[1] // count
    copies = []
    for part in range(parts):
        for k in range(count):
            rows = blocks[part * count + k].shape[0]
            at = pl.multiple_of(meta[k] * block, block)
            copies.append(
                pltpu.make_async_copy(
                    blocks[part * count + k],
                    held.at[pl.ds(part * rows, rows), pl.ds(at, block)],
                    sems.at[len(copies)],
                )
            )
    for copy in copies:
        copy.start()
    for copy in copies:
        copy.wait()


def held_dot(held, weights):
    total, at = None, 0
    for weight in weights:
        term = jnp.dot(held[:, at : at + weight.shape[0]], weight, preferred_element_type=F32)
        total = term if total is None else total + term
        at += weight.shape[0]
    return total


def state_kernel(nblocks, meta, *refs):
    blocks, refs = refs[:nblocks], refs[nblocks:]
    key_own, value_own, key_sib, value_sib = refs[:4]
    key_far, value_far = refs[4:6], refs[6:8]
    out, rounded, held, sems = refs[8:]
    prompts = out.shape[0]
    half = nblocks // 2

    @pl.when(pl.program_id(0) == 0)
    def _():
        parts = [blocks[s * half + k].at[p] for p in range(prompts) for s in range(2) for k in range(half)]
        fetch_rows(meta, parts, 2 * prompts, held, sems)

    keys = [key_own[0], key_sib[0]] + [ref[...] for ref in key_far]
    values = [value_own[0], value_sib[0]] + [ref[...] for ref in value_far]
    parts = [jnp.concatenate(pair, axis=1) for pair in zip(keys, values)]
    both = held_dot(held, parts).astype(BF16)
    tokens = both.shape[0] // prompts
    for p in range(prompts):
        rows = both[p * tokens : (p + 1) * tokens]
        state = lax.dot_general(
            rows[:, :DH], rows[:, DH:], (((0,), (0,)), ((), ())), preferred_element_type=F32
        )
        out[p, 0] = state
        rounded[p, 0] = state.astype(BF16)


def project_kernel(nhead, steps, meta, *refs):
    mine, other, refs = refs[:nhead], refs[nhead : 2 * nhead], refs[2 * nhead :]
    own, sib = refs[:3], refs[3:6]
    far = refs[6:8], refs[8:10], refs[10:12]
    rows_out, residual, held = refs[12:]
    rows, block = held.shape[1:]
    features = nhead * block

    @pl.when(pl.program_id(0) == 0)
    def _():
        for k in range(nhead):
            held[meta[k], : rows // 2] = mine[k][...]
            held[meta[k], rows // 2 :] = other[k][...]
        share = residual.shape[0]
        at = pl.multiple_of(meta[nhead] * share, share)
        for j in range(nhead):
            residual[:, j * block : (j + 1) * block] = held[j, pl.ds(at, share), :]

    blocks = [held[j] for j in range(nhead)]

    squares = jnp.zeros((rows, 1), F32)
    for part in blocks:
        part = part.astype(F32)
        squares += jnp.sum(part * part, axis=-1, keepdims=True)
    scale = lax.rsqrt(squares / features + 1e-06)

    total = None
    for j, part in enumerate(blocks):
        each = [(own[i][0], sib[i][0], far[i][0][...], far[i][1][...])[j] for i in range(3)]
        term = jnp.dot(part, jnp.concatenate(each, axis=1), preferred_element_type=F32)
        total = term if total is None else total + term
    total = (total * scale).astype(BF16)
    wide = total.shape[1] // 3
    query, key, value = (total[:, i * wide : (i + 1) * wide] for i in range(3))
    width = query.shape[1]
    rows_out[:, :width] = query.astype(F32)
    query, key, value = query.astype(F32), key.astype(F32), value.astype(F32)
    each = rows // 2 // steps
    for part in range(2):
        for s in range(steps):
            at_s = slice((part * steps + s) * each, (part * steps + s + 1) * each)
            for head in range(query.shape[1] // DH):
                cols = slice(head * DH, (head + 1) * DH)
                total = None
                for u in range(s + 1):
                    at_u = slice((part * steps + u) * each, (part * steps + u + 1) * each)
                    score = jnp.sum(query[at_s, cols] * key[at_u, cols], axis=-1, keepdims=True)
                    term = score.astype(BF16).astype(F32) * value[at_u, cols]
                    total = term if total is None else total + term
                rows_out[at_s, width + head * DH : width + (head + 1) * DH] = total


def attend_kernel(wide, arrived, chosen, states, others, out, given):
    second = chosen[...] != 0
    rows = out.shape[0]
    for head in range(states.shape[1]):
        cols = slice(head * DH, (head + 1) * DH)
        at = 2 * wide * (head * DH // wide) + head * DH % wide
        q = arrived[:, at : at + DH].astype(BF16)
        both = []
        for p in range(2):
            state = states[p, head] + others[p, head].astype(F32)
            high = state.astype(BF16)
            low = (state - high.astype(F32)).astype(BF16)
            both.append(
                jnp.dot(q, high, preferred_element_type=F32) + jnp.dot(q, low, preferred_element_type=F32)
            )
        attended = jnp.where(second, both[1], both[0]) + arrived[:, at + wide : at + wide + DH]
        normed = rms_rows(attended).astype(BF16)
        out[:, cols] = normed[:rows]
        given[:, cols] = normed[rows:]


def share_out(meta, terms, outs):
    for k, out in enumerate(outs):
        share = out.shape[0]
        at = pl.multiple_of(meta[k] * share, share)
        out[...] = terms[pl.ds(at, share), :].astype(out.dtype)


def near_kernel(meta, heads_own, heads_sib, own, sib, *refs):
    outs, terms = refs[:-1], refs[-1]
    core = meta[len(outs)]
    half, width = heads_own.shape[1], own.shape[1]
    own_at = pl.multiple_of(core * half, half)
    sib_at = pl.multiple_of((1 - core) * half, half)
    for j, weight in enumerate((own, sib)):
        term = jnp.dot(heads_own[...], weight[pl.ds(own_at, half), :], preferred_element_type=F32)
        term += jnp.dot(heads_sib[...], weight[pl.ds(sib_at, half), :], preferred_element_type=F32)
        terms[:, j * width : (j + 1) * width] = term
    share_out(meta, terms, outs)


def far_kernel(meta, heads_own, heads_sib, far_x, far_y, diag_x, diag_y, *refs):
    outs, heads, terms = refs[:-2], refs[-2], refs[-1]
    core, group = meta[len(outs)], meta[len(outs) + 1]
    heads[core] = heads_own[...]
    heads[1 - core] = heads_sib[...]
    width = far_x.shape[1]
    for i, (first, second) in enumerate(((far_x, far_y), (diag_x, diag_y))):
        term = jnp.dot(heads[group], first[...], preferred_element_type=F32)
        term += jnp.dot(heads[1 - group], second[...], preferred_element_type=F32)
        at = pl.multiple_of((i ^ group) * width, width)
        terms[:, pl.ds(at, width)] = term
    share_out(meta, terms, outs)


def norm_kernel(nhead, meta, residual, *refs):
    near, far, outs, mixed = refs[:nhead], refs[nhead : 2 * nhead], refs[2 * nhead : 3 * nhead], refs[-1]
    part = near[0].shape[1]
    squares = 0.0
    for i, group in enumerate((near, far)):
        total = residual[:, i * part : (i + 1) * part].astype(F32)
        for ref in group:
            total = total + ref[...].astype(F32)
        squares = squares + jnp.sum(total * total, axis=-1, keepdims=True)
        width = outs[0].shape[1]
        for j in range(part // width):
            mixed[i * (part // width) + j] = total[:, j * width : (j + 1) * width]
    scale = lax.rsqrt(squares / (2 * part) + 1e-06)
    for k, out in enumerate(outs):
        out[...] = (mixed[meta[k]] * scale).astype(out.dtype)


def place_kernel(meta, *refs):
    out = refs[-1]
    for k, piece in enumerate(refs[:-1]):
        share = piece.shape[0]
        out[pl.ds(pl.multiple_of(meta[k] * share, share), share), :] = piece[...]


def anywhere(count):
    return [pl.BlockSpec(memory_space=pltpu.HBM)] * count


def in_vmem(count):
    return [pl.BlockSpec(memory_space=pltpu.VMEM)] * count


def small_call(kernel, name, meta, operands, outs, scratch=(), flops=0, limit=VMEM_SMALL):
    return pl.pallas_call(
        kernel,
        out_shape=outs,
        grid_spec=pltpu.PrefetchScalarGridSpec(
            num_scalar_prefetch=1,
            grid=(),
            in_specs=in_vmem(len(operands)),
            out_specs=tuple(in_vmem(len(outs))) if isinstance(outs, tuple) else in_vmem(1)[0],
            scratch_shapes=list(scratch),
        ),
        compiler_params=pltpu.CompilerParams(vmem_limit_bytes=limit),
        cost_estimate=pl.CostEstimate(flops=flops, bytes_accessed=4 * 1024 * 1024, transcendentals=0),
        name=name,
    )(meta, *operands)


def permuted_plan(prompt_hidden, qkv_weight, out_weight, embed_table, response_ids, assignment):
    grp, ctx, head = lax.axis_index("grp"), lax.axis_index("ctx"), lax.axis_index("head")
    nctx, nhead = lax.axis_size("ctx"), lax.axis_size("head")
    core, chip = ctx % 2, ctx // 2
    to_sib, to_far = xor_pairs(nctx, 1), xor_pairs(nctx, 2)
    fetch = [(g * nctx + c, g * nctx + (c ^ (2 + g))) for g in range(2) for c in range(nctx)]
    ring = shift_pairs(nhead, 1)
    prompts, prompt_rows, block = prompt_hidden.shape
    depth = block // 2
    cols = qkv_weight.shape[2] // 2
    steps = response_ids.shape[0]
    resp_local = response_ids.shape[1] // nctx
    rows_local = steps * resp_local

    sib = lambda array: permute(array, "ctx", to_sib)
    up = lambda array: permute(array, "head", ring)
    swap = lambda array: permute(array, "grp", xor_pairs(2, 1))

    def lookup(ids):
        offset_ids = ids - ctx * embed_table.shape[0]
        return jnp.take(embed_table, jnp.clip(offset_ids, 0, embed_table.shape[0] - 1), axis=0)

    def by_core(looked):
        vocab_rows = embed_table.shape[0]
        offset_ids = response_ids - ctx * vocab_rows
        inside = (offset_ids >= 0) & (offset_ids < vocab_rows)
        looked = jnp.where(inside[:, :, None], looked, jnp.zeros((), BF16))
        looked = looked.reshape(steps, nctx // 2, 2, resp_local, block)
        kept = lax.dynamic_index_in_dim(looked, core, 2, keepdims=False)
        given = lax.dynamic_index_in_dim(looked, 1 - core, 2, keepdims=False)

        def halves(received):
            total = kept + received
            mine = lax.dynamic_index_in_dim(total, chip, 1, keepdims=False)
            given = lax.dynamic_index_in_dim(total, 1 - chip, 1, keepdims=False)
            return mine.reshape(rows_local, block), given.reshape(rows_local, block)

        return given, halves

    width = out_weight.shape[1]
    tie = lax.optimization_barrier

    def fetched(k, weight):
        return lax.dynamic_slice(weight, (k, 0, (core ^ grp) * cols), (1, block, cols))[0]

    def cross(array):
        return permute(array, ("grp", "ctx"), fetch)

    places = []
    for k in range(nhead):
        place = ctx ^ ((head - k) % nhead)
        places.append(jnp.where(place < 2, place, place ^ grp))
    meta = jnp.stack(places + [head, core, grp]).astype(jnp.int32)
    at_core = nhead + 1

    ahead = [(head + k) % nhead for k in range(nhead)]
    out_meta = jnp.stack(ahead + [core, grp]).astype(jnp.int32)
    norm_meta = [ctx ^ f for f in ahead]
    norm_meta = jnp.stack([jnp.where(j < 2, j, j ^ grp) for j in norm_meta]).astype(jnp.int32)
    behind = jnp.stack([(head - k) % nhead for k in range(nhead)]).astype(jnp.int32)
    which = [
        jnp.tile(lax.dynamic_slice_in_dim(assignment, owner * resp_local, resp_local, 0), steps)
        for owner in (ctx, ctx ^ 1)
    ]
    chosen = jnp.concatenate(which)[:, None]

    first_half, later_weight, prompt_hidden = tie((fetched(1, qkv_weight), qkv_weight, prompt_hidden))
    tokens = [prompt_hidden, up(prompt_hidden)]
    keys_x = cross(first_half)
    sib_tokens = [sib(prompt_hidden)]
    sib_weight = sib(later_weight)
    out_sib = sib(out_weight)
    next_half, ids, later_weight = tie((fetched(2, later_weight), response_ids, later_weight))
    given, halves_of = by_core(lookup(ids))

    metas = (meta, out_meta, norm_meta, behind, chosen)
    query_half = fetched(0, later_weight)
    next_half, tokens, keys_x, sib_tokens, sib_weight, given, query_half, metas, out_sib = tie(
        (next_half, tokens, keys_x, sib_tokens, sib_weight, given, query_half, metas, out_sib)
    )
    meta, out_meta, norm_meta, behind, chosen = metas
    values_x = cross(next_half)
    tokens.append(up(tokens[1]))
    keys_y = swap(keys_x)
    sib_tokens.append(sib(tokens[1]))
    mine, given = halves_of(sib(given))
    given = permute(given, "ctx", to_far)

    query_x = cross(query_half)
    values_x, tokens, keys_y, sib_tokens, mine = tie((values_x, tokens, keys_y, sib_tokens, mine))
    tokens.append(up(tokens[2]))
    values_y = swap(values_x)
    sib_tokens.append(sib(tokens[2]))
    embedded = mine + given
    out_half = lax.dynamic_slice(out_weight, (grp * depth, 0), (depth, width))

    tokens, query_x, values_y, sib_tokens, embedded, out_half = tie(
        (tokens, query_x, values_y, sib_tokens, embedded, out_half)
    )
    out_x = permute(out_half, "ctx", to_far)
    query_y = swap(query_x)
    e = [embedded] + [permute(embedded, "head", shift_pairs(nhead, k)) for k in range(1, nhead)]
    sib_tokens.append(sib(tokens[3]))

    def own_spec(k, wide):
        return pl.BlockSpec((1, block, wide), lambda n, m: (k, 0, m[at_core] * (cols // wide) + n))

    sib_spec = own_spec

    def far_spec(wide):
        return pl.BlockSpec((block, wide), lambda n, m: (0, n))

    crossed = ((query_x, query_y), (keys_x, keys_y), (values_x, values_y))
    far_of = lambda k: crossed[k]
    nblocks = 2 * nhead
    heads_here = cols // DH
    chip_tokens = 2 * prompts * prompt_rows

    state_spec = pl.BlockSpec((prompts, 1, DH, DH), lambda n, m: (0, n, 0, 0))
    states, rounded = pl.pallas_call(
        functools.partial(state_kernel, nblocks),
        out_shape=(
            jax.ShapeDtypeStruct((prompts, heads_here, DH, DH), F32),
            jax.ShapeDtypeStruct((prompts, heads_here, DH, DH), BF16),
        ),
        grid_spec=pltpu.PrefetchScalarGridSpec(
            num_scalar_prefetch=1,
            grid=(heads_here,),
            in_specs=anywhere(nblocks)
            + [own_spec(1, DH), own_spec(2, DH), sib_spec(1, DH), sib_spec(2, DH)]
            + [far_spec(DH)] * 4,
            out_specs=(state_spec, state_spec),
            scratch_shapes=[
                pltpu.VMEM((chip_tokens, nhead * block), BF16),
                pltpu.SemaphoreType.DMA((prompts * nblocks,)),
            ],
        ),
        compiler_params=pltpu.CompilerParams(vmem_limit_bytes=VMEM_LIMIT),
        cost_estimate=pl.CostEstimate(
            flops=4 * chip_tokens * nhead * block * cols, bytes_accessed=16 * 1024 * 1024, transcendentals=0
        ),
        name="prompt_state",
    )(
        meta,
        *tokens,
        *sib_tokens,
        qkv_weight,
        qkv_weight,
        sib_weight,
        sib_weight,
        *far_of(1),
        *far_of(2),
    )

    states, rounded, e = tie((states, rounded, e))
    sib_e = [sib(array) for array in e]
    others = permute(rounded, "ctx", to_far)
    states, out_x, query_y, query_x = tie((states, out_x, query_y, query_x))
    out_y = swap(out_x)

    chip_rows = 2 * rows_local
    share = rows_local // nhead
    wide = 2 * DH
    row_spec = pl.BlockSpec((chip_rows, 2 * wide), lambda n, m: (0, n))
    rows_out, residual = pl.pallas_call(
        functools.partial(project_kernel, nhead, steps),
        out_shape=(
            jax.ShapeDtypeStruct((chip_rows, 2 * cols), F32),
            jax.ShapeDtypeStruct((share, nhead * block), BF16),
        ),
        grid_spec=pltpu.PrefetchScalarGridSpec(
            num_scalar_prefetch=1,
            grid=(cols // wide,),
            in_specs=[pl.BlockSpec((rows_local, block), lambda n, m: (0, 0))] * nblocks
            + [own_spec(k, wide) for k in range(3)]
            + [sib_spec(k, wide) for k in range(3)]
            + [far_spec(wide)] * 6,
            out_specs=(row_spec, pl.BlockSpec((share, nhead * block), lambda n, m: (0, 0))),
            scratch_shapes=[pltpu.VMEM((nhead, chip_rows, block), BF16)],
        ),
        compiler_params=pltpu.CompilerParams(vmem_limit_bytes=VMEM_LIMIT),
        cost_estimate=pl.CostEstimate(
            flops=6 * chip_rows * nhead * block * cols, bytes_accessed=14 * 1024 * 1024, transcendentals=0
        ),
        name="response_rows",
    )(
        meta,
        *e,
        *sib_e,
        *([qkv_weight] * 3),
        *([sib_weight] * 3),
        *far_of(0),
        *far_of(1),
        *far_of(2),
    )

    heads_own, heads_sib = pl.pallas_call(
        functools.partial(attend_kernel, wide),
        out_shape=(jax.ShapeDtypeStruct((rows_local, cols), BF16),) * 2,
        compiler_params=pltpu.CompilerParams(vmem_limit_bytes=VMEM_SMALL),
        name="attend",
    )(rows_out, chosen, states, others)
    heads_sib = sib(heads_sib)

    def spread(kernel, name, heads, operands, scratch):
        outs = (jax.ShapeDtypeStruct((share, 2 * width), F32),)
        outs += (jax.ShapeDtypeStruct((share, 2 * width), BF16),) * (nhead - 1)
        scratch = [*scratch, pltpu.VMEM((rows_local, 2 * width), F32)]
        flops = 4 * rows_local * block * width
        terms = small_call(kernel, name, out_meta, (*heads, *operands), outs, scratch, flops)
        moved = {k: permute(terms[k], "head", shift_pairs(nhead, k)) for k in (2, 3, 1)}
        return [terms[0]] + [moved[k] for k in range(1, nhead)]

    near = spread(near_kernel, "near_terms", (heads_own, heads_sib), (out_weight, out_sib), [])
    heads_own, heads_sib, out_y = tie((heads_own, heads_sib, out_y, near[2]))[:3]
    diag_x = sib(out_x)
    far = spread(
        far_kernel,
        "far_terms",
        (heads_own, heads_sib),
        (out_x, out_y, diag_x, sib(out_y)),
        [pltpu.VMEM((2, rows_local, cols), BF16)],
    )
    normed = small_call(
        functools.partial(norm_kernel, nhead),
        "final_norm",
        norm_meta,
        (residual, *near, *far),
        (jax.ShapeDtypeStruct((share, width), BF16),) * nhead,
        [pltpu.VMEM((nhead, share, width), F32)],
    )
    pieces = [normed[0]] + [permute(normed[k], "head", shift_pairs(nhead, k)) for k in range(1, nhead)]
    result = small_call(
        place_kernel, "place", behind, pieces, jax.ShapeDtypeStruct((rows_local, width), BF16)
    )
    return result.reshape(steps, resp_local, width)


def on_device(prompt_hidden, qkv_weight, out_weight, embed_table, response_ids, assignment):
    nctx, nhead = lax.axis_size("ctx"), lax.axis_size("head")
    local_heads = qkv_weight.shape[2] // DH
    fits = (
        lax.axis_size("grp") == 2
        and nctx == 4
        and nhead == 4
        and prompt_hidden.shape[0] == 2
        and local_heads % 4 == 0
        and prompt_hidden.shape[1] % 16 == 0
        and (response_ids.shape[1] // nctx) % (16 * nhead // response_ids.shape[0]) == 0
        and (response_ids.shape[1] // nctx) % 16 == 0
    )
    plan = permuted_plan if fits else gathered_plan
    return plan(prompt_hidden, qkv_weight, out_weight, embed_table, response_ids, assignment)


def solution(mesh):
    return jax.shard_map(
        on_device,
        mesh=mesh,
        in_specs=(
            P("grp", "ctx", "head"),
            P(None, "ctx", "head"),
            P("head", "ctx"),
            P("ctx", "head"),
            P(None, "grp"),
            P("grp"),
        ),
        out_specs=P(None, ("grp", "ctx"), "head"),
        check_vma=False,
    )
```
